512 devices in a mesh: rep: 32 (over y, z_hi), shard: 16 (over z_lo, x, core).
Axes of the slice: x: 4, y: 8, z: 8 (z_hi: 4, z_lo: 2; z = z_hi * 2 + z_lo), core: 2. Of those that a mesh axis runs over, the one named last changes fastest.
Arguments:
- grad: bfloat16 [8192, 2048], P('shard'), may hold values from -1.5 to 1.5
- owner: int32 [32, 8], replicated, may hold values from 0 to 15, as said below
- left_basis: bfloat16 [256, 256, 256], P('shard', 'rep'), may hold values from -0.375 to 0.375
- right_basis: bfloat16 [256, 256, 256], P('shard', 'rep'), may hold values from -0.375 to 0.375
- avg: bfloat16 [256, 256, 256], P('shard', 'rep'), may hold values from -1.5 to 1.5
- avg_sq: float32 [256, 256, 256], P('shard', 'rep'), may hold values from 0.002 to 0.1
- left_gram: float32 [256, 256, 256], P('shard', 'rep'), may hold values from -6 to 6
- right_gram: float32 [256, 256, 256], P('shard', 'rep'), may hold values from -6 to 6
Outputs:
- update: bfloat16 [8192, 2048], P('shard')
- new_avg: bfloat16 [256, 256, 256], P('shard', 'rep')
- new_avg_sq: float32 [256, 256, 256], P('shard', 'rep')
- new_left_gram: float32 [256, 256, 256], P('shard', 'rep')
- new_right_gram: float32 [256, 256, 256], P('shard', 'rep')
The draws below stay inside these ranges and needn't reach their ends.
Inputs may be any that keep to these rules, and one draw needn't show every extreme that they name: Each shard owns exactly 16 blocks; of the 16 blocks in one shard's rows, at most 2 share an owner, and in every shard's rows exactly 2 blocks share one owner.
All inputs are finite; a program needn't handle non-finite values.
Results may differ from the reference program's by a relative error of at most 0.0059.
Values may be sent and summed in bfloat16 or wider, within the bound.
A program may use at most 64 MiB of HBM per device.

```python
import math
import jax
import jax.numpy as jnp
from jax import lax

B = 256
RPS = 2
CB = 8
BR = 32
KB = 16
NBLK = 256
ROWS = 8192
COLS = 2048
N_SHARD = 16


def draw_owner(key, part):
    key = jax.random.fold_in(key, 11)
    count = BR // RPS
    key_base, key_label, key_order = jax.random.split(key, 3)
    base = jax.random.permutation(key_base, count)
    offsets = jnp.concatenate([base[:1], base[:-1]])
    labels = jax.random.permutation(key_label, count)
    orders = jax.vmap(lambda single: jax.random.permutation(single, count))(jax.random.split(key_order, count))
    shifted = offsets[orders]
    source = jnp.arange(count, dtype=jnp.int32)[:, None]
    owners = labels[(source + shifted) % count]
    return owners.reshape(BR, CB).astype(jnp.int32)


def shard_levels(rng, extent, shards, least, high):
    factor_of, own = 1.0, jax.random.fold_in(rng, 6)
    for dim, blocks in shards:
        steps = jnp.exp(jax.random.uniform(jax.random.fold_in(own, dim), (blocks,), jnp.float32, least / len(shards), high / len(shards)))
        factor_of = factor_of * jnp.repeat(steps, extent[dim] // blocks).reshape([-1 if axis == dim else 1 for axis in range(len(extent))])
    return factor_of


def bell_draw(stream_key, dims, spread, reach, cuts=(), kind=jnp.bfloat16):
    gain = shard_levels(stream_key, dims, cuts, -0.22, 0.18) if cuts else 1.0
    drawn = jax.random.normal(stream_key, dims, jnp.float32) * spread * gain
    return jnp.minimum(jnp.maximum(drawn, -reach), reach).astype(kind)


def setup_inputs(seed: int = 0) -> dict:
    seeds = jax.random.split(jax.random.key(seed), 9)
    grad = bell_draw(seeds[0], (ROWS, COLS), 0.25, 1.5, ((0, 16),))
    owner = draw_owner(jax.random.fold_in(seeds[8], 71), 0)
    left_basis = bell_draw(seeds[2], (NBLK, B, B), B ** -0.5, 0.375, ((0, 16), (1, 32)))
    right_basis = bell_draw(seeds[3], (NBLK, B, B), B ** -0.5, 0.375, ((0, 16), (1, 32)))
    avg = bell_draw(seeds[4], (NBLK, B, B), 0.25, 1.5, ((0, 16), (1, 32)))
    avg_sq = jnp.clip(jnp.exp(math.log(0.1) - 3.912023 * jax.random.uniform(seeds[5], (NBLK, B, B), jnp.float32) ** shard_levels(seeds[5], (NBLK, B, B), ((0, 16), (1, 32)), -0.2, 0.2)), 0.002, 0.1)
    left_gram = bell_draw(seeds[6], (NBLK, B, B), 1.0, 6.0, ((0, 16), (1, 32)), jnp.float32)
    right_gram = bell_draw(seeds[7], (NBLK, B, B), 1.0, 6.0, ((0, 16), (1, 32)), jnp.float32)
    return {"grad": grad, "owner": owner, "left_basis": left_basis, "right_basis": right_basis, "avg": avg, "avg_sq": avg_sq, "left_gram": left_gram, "right_gram": right_gram}


BETA_ONE = 0.9
BETA_TWO = 0.95
EPSILON = 1e-08

def state_index(owner):
    flat = owner.reshape(-1).astype(jnp.int32)
    hits = (flat[:, None] == jnp.arange(N_SHARD, dtype=jnp.int32)[None, :]).astype(jnp.int32)
    ranks = lax.optimization_barrier(jnp.sum((jnp.cumsum(hits, axis=0) - hits) * hits, axis=1))
    return (flat * KB + ranks).astype(jnp.int32)

def reference(grad, owner, left_basis, right_basis, avg, avg_sq, left_gram, right_gram):
    index = state_index(owner)
    blocks = grad.reshape(BR, B, CB, B).transpose(0, 2, 1, 3).reshape(NBLK, B, B).astype(jnp.float32)
    eigen = left_basis[index].astype(jnp.float32)
    rotate = right_basis[index].astype(jnp.float32)
    half = jnp.einsum('kab,kbc->kac', eigen, blocks).astype(jnp.bfloat16)
    turned = jnp.einsum('kac,kcd->kad', half.astype(jnp.float32), rotate)
    first = BETA_ONE * avg[index].astype(jnp.float32) + (1.0 - BETA_ONE) * turned
    second = BETA_TWO * avg_sq[index] + (1.0 - BETA_TWO) * turned * turned
    scaled = (first / (jnp.sqrt(second) + EPSILON)).astype(jnp.bfloat16)
    back = jnp.einsum('kad,ked->kae', scaled.astype(jnp.float32), rotate).astype(jnp.bfloat16)
    summed = jnp.einsum('kab,kac->kbc', eigen, back.astype(jnp.float32))
    update = summed.astype(jnp.bfloat16).reshape(BR, CB, B, B).transpose(0, 2, 1, 3).reshape(ROWS, COLS)
    left_new = BETA_TWO * left_gram[index] + (1.0 - BETA_TWO) * jnp.einsum('kab,kcb->kac', blocks, blocks)
    right_new = BETA_TWO * right_gram[index] + (1.0 - BETA_TWO) * jnp.einsum('kba,kbc->kac', blocks, blocks)
    new_avg = jnp.zeros((NBLK, B, B), jnp.bfloat16).at[index].set(first.astype(jnp.bfloat16))
    new_avg_sq = jnp.zeros((NBLK, B, B), jnp.float32).at[index].set(second)
    new_left_gram = jnp.zeros((NBLK, B, B), jnp.float32).at[index].set(left_new)
    new_right_gram = jnp.zeros((NBLK, B, B), jnp.float32).at[index].set(right_new)
    return (update, new_avg, new_avg_sq, new_left_gram, new_right_gram)
```

```python
import functools

import jax
import jax.numpy as jnp
from jax import lax
from jax.experimental import pallas as pl
from jax.experimental.pallas import tpu as pltpu
from jax.sharding import PartitionSpec as P

CAP = 2
BETA_ONE = 0.9
BETA_TWO = 0.95
EPSILON = 1e-08

YS = 8
ZS = 4
REPS = YS * ZS
SHARDS = 16
KEPT = 16
W = 256
PR, PC = 16, 128
PARTS = 2
FAR_Y = (4, 3, 5, 2, 6, 1, 7, 0)
FAR_Z = (2, 1, 3, 0)
MESH = pl.DeviceIdType.MESH


def routing(owner, here):
    flat = owner.T.reshape(-1)
    place = jnp.arange(flat.shape[0], dtype=jnp.int32)
    ident = place % owner.shape[0] * owner.shape[1] + place // owner.shape[0]
    source = ident // KEPT
    same = (flat[:, None] == flat[None, :]) & (ident[None, :] < ident[:, None])
    rank = jnp.sum(same.astype(jnp.int32), axis=1)
    pair = jnp.sum((same & (source[:, None] == source[None, :])).astype(jnp.int32), axis=1)
    local = jnp.arange(KEPT, dtype=jnp.int32)
    slots = jnp.arange(SHARDS * CAP, dtype=jnp.int32)
    mine = (ident[None, :] == here * KEPT + local[:, None]).astype(jnp.int32)
    dest = jnp.sum(mine * (flat * CAP + pair)[None, :], axis=1)
    owned = ((flat == here)[None, :] & (rank[None, :] == local[:, None])).astype(jnp.int32)
    recv = jnp.sum(owned * (source * CAP + pair)[None, :], axis=1)
    send_pick = jnp.sum((dest[None, :] == slots[:, None]).astype(jnp.int32) * local[None, :], axis=1)
    back_pick = jnp.sum((recv[None, :] == slots[:, None]).astype(jnp.int32) * local[None, :], axis=1)
    return jnp.concatenate([send_pick, recv, back_pick, dest])


def fold(x):
    x = x.astype(jnp.float32)
    return jnp.concatenate([x[:, :, :PC], x[:, :, PC:]], axis=1).astype(jnp.bfloat16)


def unfold(x):
    x = x.astype(jnp.float32)
    return jnp.concatenate([x[:, :8, :], x[:, 8:, :]], axis=2)


def nn(a, b):
    return lax.dot_general(a, b, (((1,), (0,)), ((), ())), preferred_element_type=jnp.float32)


def nt(a, b):
    return lax.dot_general(a, b, (((1,), (1,)), ((), ())), preferred_element_type=jnp.float32)


def tn(a, b):
    return lax.dot_general(a, b, (((0,), (0,)), ((), ())), preferred_element_type=jnp.float32)


def wait_bytes(ref, sem):
    pltpu.make_async_copy(ref, ref, sem).wait()


def kernel(
    idx, left_h, right_h, avg_h, avg_sq_h, grad, left_gram_h, right_gram_h,
    update, new_avg, new_avg_sq, new_left, new_right,
    left, right, avg, avg_sq, whole, left_gram, right_gram,
    folded, bases_out, moments_out, bases_in, moments_in, bases_row, moments_row, bases, moments,
    rsend, rbuf, grams, tsend, trecv,
    load_sem, send_sem, recv_sem, z_send, ag_send, ag_recv,
):
    r = lax.axis_index("rep")
    s = lax.axis_index("shard")
    y, z = r // ZS, r % ZS
    z_half, z_odd = z // 2, z % 2
    p0 = (y + s) % 2
    is_hub = z_odd == p0

    def wrap(v, n):
        return jnp.where(v >= n, v - n, v)

    ys = [wrap(y + t, YS) for t in range(YS)]
    zs = [wrap(z + t, ZS) for t in range(ZS)]
    z_low, x, core = s // 8, s % 8 // 2, s % 2
    xs = [wrap(x + t, 4) for t in range(4)]
    ss = [
        (1 - z_low if a else z_low) * 8 + xs[b] * 2 + (1 - core if c else core)
        for a, b, c in (
            (1, 2, 1), (1, 2, 0), (0, 2, 1), (0, 2, 0), (1, 1, 1), (1, 1, 0), (1, 3, 1), (1, 3, 0),
            (0, 1, 1), (0, 1, 0), (0, 3, 1), (0, 3, 0), (1, 0, 1), (1, 0, 0), (0, 0, 1),
        )
    ]

    def to(rep):
        return dict(device_id={"rep": rep}, device_id_type=MESH)

    def over(shard):
        return dict(device_id={"shard": shard}, device_id_type=MESH)

    loads = [
        pltpu.make_async_copy(src, dst, load_sem.at[n])
        for n, (src, dst) in enumerate(
            [(left_h, left), (right_h, right), (avg_h, avg), (avg_sq_h, avg_sq),
             (grad, whole), (left_gram_h, left_gram), (right_gram_h, right_gram)]
        )
    ]
    for copy in loads[:4]:
        copy.start()

    barrier = pltpu.get_barrier_semaphore()
    for peer in ss:
        pl.semaphore_signal(barrier, inc=1, **over(peer))

    @pl.when(is_hub)
    def _():
        for t in FAR_Y[:-1]:
            for v in FAR_Z[:-1]:
                pl.semaphore_signal(barrier, inc=1, **to(ys[t] * ZS + zs[v]))

    for t in FAR_Y[:-1]:
        pl.semaphore_signal(barrier, inc=1, **to(ys[t] * ZS + z))
    for v in FAR_Z[:-1]:
        pl.semaphore_signal(barrier, inc=1, **to(y * ZS + zs[v]))

    for n, ref in enumerate((left, right, avg, avg_sq)):
        loads[n].wait()
        folded[:, n] = fold(ref[...])
    for n in range(SHARDS * CAP):
        block = folded[idx[SHARDS * CAP + KEPT + n]]
        bases_out[n] = block[:2]
        moments_out[n] = block[2:]
    pl.semaphore_wait(barrier, jnp.where(is_hub, SHARDS - 1 + 21, SHARDS - 1 + 20))

    mine = pl.ds(s * CAP, CAP)

    def exchange(src, dst, n):
        pltpu.make_async_copy(src.at[mine], dst.at[mine], recv_sem.at[n]).start()
        for peer in ss:
            pltpu.make_async_remote_copy(
                src.at[pl.ds(peer * CAP, CAP)], dst.at[mine], send_sem.at[n], recv_sem.at[n], **over(peer)
            ).start()

    exchange(bases_out, bases_in, 0)
    exchange(moments_out, moments_in, 1)
    for copy in loads[4:]:
        copy.start()

    def to_hub(src, dst, n):
        for t in FAR_Y:
            p = p0 if t % 2 == 0 else 1 - p0
            for b in (1 - z_half, z_half):
                block, h = 2 * ys[t] + b, ys[t] * ZS + 2 * b + p

                def remote(block=block, h=h):
                    pltpu.make_async_remote_copy(
                        src.at[block], dst.at[r], send_sem.at[n], recv_sem.at[n], **to(h)
                    ).start()

                if t == 0:
                    pl.when(h != r)(remote)

                    @pl.when(h == r)
                    def _(block=block):
                        pltpu.make_async_copy(src.at[block], dst.at[r], recv_sem.at[n]).start()
                else:
                    remote()

    for n, (got, row, out) in enumerate(
        ((bases_in, bases_row, bases), (moments_in, moments_row, moments))
    ):
        wait_bytes(got, recv_sem.at[n])
        for b in range(KEPT):
            row[b] = got[idx[2 * SHARDS * CAP + KEPT + b]]
        to_hub(row, out, 2 + n)

    block_me = 2 * y + z_half
    row_of = [pl.multiple_of(ys[t] // 4 * W, W) for t in range(YS)]
    col_of = [pl.multiple_of(ys[t] % 4 * (2 * W), W) for t in range(YS)]

    @pl.when(is_hub)
    def _():
        loads[4].wait()
        here = (pl.ds(row_of[0], W), pl.ds(pl.multiple_of(col_of[0] + z_half * W, W), W))
        g = whole[here]
        wait_bytes(bases, recv_sem.at[2])
        lb = unfold(bases[:, 0]).reshape(W, W).astype(jnp.bfloat16)
        rb = unfold(bases[:, 1]).reshape(W, W).astype(jnp.bfloat16)
        half = nn(lb, g).astype(jnp.bfloat16)
        turned = nn(half, rb)
        wait_bytes(moments, recv_sem.at[3])
        m0 = unfold(moments[:, 0]).reshape(W, W)
        v0 = unfold(moments[:, 1]).reshape(W, W)
        first = BETA_ONE * m0 + (1.0 - BETA_ONE) * turned
        second = BETA_TWO * v0 + (1.0 - BETA_TWO) * turned * turned
        scaled = (first / (jnp.sqrt(second) + EPSILON)).astype(jnp.bfloat16)
        back = nt(scaled, rb).astype(jnp.bfloat16)
        update[here] = tn(lb, back).astype(jnp.bfloat16)
        rsend[...] = fold(turned.reshape(REPS, 8, W))

    ups = (ys[1] * ZS + z, ys[7] * ZS + z)
    z_pair = 2 * z_half + 1 - z_odd
    z_next = jnp.where(z_odd == 1, zs[1], zs[3])
    pending = []
    names = {}

    def region(t, bit, rows):
        return update.at[
            pl.ds(pl.multiple_of(row_of[t] + rows[0], 16), rows[1] - rows[0]),
            pl.ds(pl.multiple_of(col_of[t] + bit * W, W), W),
        ]

    def push(ref, peer, key):
        n = names.setdefault(key, len(names))
        copy = pltpu.make_async_remote_copy(ref, ref, ag_send.at[n], ag_recv.at[n], **to(peer))
        copy.start()
        return copy

    def pull(ref, key):
        wait_bytes(ref, ag_recv.at[names[key]])

    bits = (z_half, 1 - z_half)
    parts = [(n * W // PARTS, (n + 1) * W // PARTS) for n in range(PARTS)]

    @pl.when(is_hub)
    def _():
        for m, rows in enumerate(parts):
            ref = region(0, bits[0], rows)
            for n, (c, peer) in enumerate(((1, zs[2]), (1, z_next), (0, z_pair))):
                key = names.setdefault(("z", c, m), len(names))
                pltpu.make_async_remote_copy(
                    ref, ref, z_send.at[3 * m + n], ag_recv.at[key], **to(y * ZS + peer)
                ).start()

    def y_rows(m, d, way):
        lo, hi = parts[m]
        if d < YS // 2:
            return lo, hi
        mid = (lo + hi) // 2
        return (lo, mid) if way == 0 else (mid, hi)

    def far(d, way):
        return (-d if way == 0 else d) % YS

    def y_push(c, m, d, way):
        ref = region(far(d - 1, way), bits[c], y_rows(m, d, way))
        pending.append(push(ref, ups[way], ("y", c, m, d, way)))

    def z_step(c, m):
        ref = region(0, bits[c], parts[m])
        if c == 0:
            pl.when(jnp.logical_not(is_hub))(lambda: pull(ref, ("z", c, m)))
        else:
            pull(ref, ("z", c, m))
        for way in range(2):
            y_push(c, m, 1, way)

    def y_step(c, m, d):
        for way in range(2):
            pull(region(far(d, way), bits[c], y_rows(m, d, way)), ("y", c, m, d, way))
            if d < YS // 2:
                y_push(c, m, d + 1, way)

    strip_at = pl.multiple_of(PR * (2 * y + z_half), PR)
    picks = (
        lax.broadcasted_iota(jnp.int32, (PR, W), 1)
        == lax.broadcasted_iota(jnp.int32, (PR, W), 0) + strip_at
    ).astype(jnp.float32).astype(jnp.bfloat16)

    def gram_rows(blocks):
        for b in blocks:
            i, j = b // 8, b % 8
            g = whole[i * W : (i + 1) * W, j * W : (j + 1) * W]
            strip = whole[pl.ds(i * W + strip_at, PR), j * W : (j + 1) * W]
            both = nt(jnp.concatenate([strip, picks], axis=0), g)
            wide = nn(both[PR:].astype(jnp.bfloat16), g)
            for n, v in enumerate((both[:PR], wide)):
                v = jnp.where(z_odd == 1, v[8:], v[:8])
                grams[b, n] = jnp.concatenate([v[:, :PC], v[:, PC:]], axis=0).astype(jnp.bfloat16)

    def side(n):
        if n == 0:

            @pl.when(jnp.logical_not(is_hub))
            def _():
                loads[4].wait()

        if n < YS // 2:

            @pl.when(is_hub)
            def _():
                for t in FAR_Y[2 * n : 2 * n + 2]:
                    for v in FAR_Z:
                        q = ys[t] * ZS + zs[v]
                        if t or v:
                            pltpu.make_async_remote_copy(
                                rsend.at[q], rbuf.at[block_me], send_sem.at[4], recv_sem.at[4], **to(q)
                            ).start()
                        else:
                            pltpu.make_async_copy(rsend.at[r], rbuf.at[block_me], recv_sem.at[4]).start()

        if n < KEPT // 2:
            gram_rows((2 * n, 2 * n + 1))
        elif n == KEPT // 2:
            wait_bytes(rbuf, recv_sem.at[4])
            for m in range(SHARDS * CAP):
                b = idx[m]
                tsend[m, 0] = rbuf[b]
                tsend[m, 1:] = grams[b]
            exchange(tsend, trecv, 5)

    def own_rows():
        wait_bytes(trecv, recv_sem.at[5])
        for copy in loads[5:]:
            copy.wait()
        for n in range(KEPT):
            turned, gl, gr = unfold(trecv[idx[SHARDS * CAP + n]])
            new_avg[n] = (BETA_ONE * avg[n].astype(jnp.float32) + (1.0 - BETA_ONE) * turned).astype(jnp.bfloat16)
            new_avg_sq[n] = BETA_TWO * avg_sq[n] + (1.0 - BETA_TWO) * turned * turned
            new_left[n] = BETA_TWO * left_gram[n] + (1.0 - BETA_TWO) * gl
            new_right[n] = BETA_TWO * right_gram[n] + (1.0 - BETA_TWO) * gr

    order = [(z_step, 0, m) for m in range(PARTS)]
    for m in range(PARTS):
        order += [(z_step, 1, m), (y_step, 0, m, 1)]
    order += [(y_step, 1, m, 1) for m in range(PARTS)]
    for d in (2, 3, 4):
        order += [(y_step, c, m, d) for c in range(2) for m in range(PARTS)]
    count = 0
    for step, *args in order[:-2]:
        step(*args)
        if count <= KEPT // 2:
            side(count)
        count += 1
        if count == len(order) - 4:
            own_rows()

    for copy in pending:
        copy.wait_send()
    for n, ref in ((0, bases_out), (1, moments_out), (5, tsend)):
        wait_bytes(ref.at[pl.ds(0, CAP * (SHARDS - 1))], send_sem.at[n])

    @pl.when(is_hub)
    def _():
        wait_bytes(bases_row.at[pl.ds(0, KEPT - 1)], send_sem.at[2])
        wait_bytes(moments_row.at[pl.ds(0, KEPT - 1)], send_sem.at[3])
        wait_bytes(rsend.at[pl.ds(0, REPS - 1)], send_sem.at[4])
        for n in range(3 * PARTS):
            wait_bytes(region(0, bits[0], parts[n // 3]), z_send.at[n])

    @pl.when(jnp.logical_not(is_hub))
    def _():
        wait_bytes(bases_row, send_sem.at[2])
        wait_bytes(moments_row, send_sem.at[3])

    for step, *args in order[-2:]:
        step(*args)


def store_kernel(*refs):
    count = len(refs) // 2
    sems = refs[-1]
    copies = []
    for n in range(count):
        src, dst = refs[n], refs[count + n]
        parts = 8 if n == 0 else 1
        size = src.shape[0] // parts
        for p in range(parts):
            rows = pl.ds(p * size, size)
            copies.append(pltpu.make_async_copy(src.at[rows], dst.at[rows], sems.at[len(copies)]))
    for copy in copies:
        copy.start()
    for copy in copies:
        copy.wait()


def body(grad, owner, left_basis, right_basis, avg, avg_sq, left_gram, right_gram):
    here = lax.axis_index("shard")
    idx = routing(owner, here)
    vmem = pl.BlockSpec(memory_space=pltpu.VMEM)
    hbm = pl.BlockSpec(memory_space=pltpu.HBM)
    bf16, f32 = jnp.bfloat16, jnp.float32
    slots = SHARDS * CAP
    rows = (KEPT, 8, W)
    outs = [jax.ShapeDtypeStruct(x.shape, x.dtype) for x in (grad, avg, avg_sq, left_gram, right_gram)]
    operands = [
        pltpu.with_memory_space_constraint(x, pltpu.HBM)
        for x in (left_basis, right_basis, avg, avg_sq, grad, left_gram, right_gram)
    ]
    results = pl.pallas_call(
        kernel,
        out_shape=outs,
        in_specs=[pl.BlockSpec(memory_space=pltpu.SMEM)] + [hbm] * 7,
        out_specs=[vmem] * 5,
        scratch_shapes=[
            pltpu.VMEM(rows, bf16),
            pltpu.VMEM(rows, bf16),
            pltpu.VMEM(rows, bf16),
            pltpu.VMEM(rows, f32),
            pltpu.VMEM(grad.shape, bf16),
            pltpu.VMEM(rows, f32),
            pltpu.VMEM(rows, f32),
            pltpu.VMEM((KEPT, 4, PR, PC), bf16),
            pltpu.VMEM((slots, 2, PR, PC), bf16),
            pltpu.VMEM((slots, 2, PR, PC), bf16),
            pltpu.VMEM((slots, 2, PR, PC), bf16),
            pltpu.VMEM((slots, 2, PR, PC), bf16),
            pltpu.VMEM((KEPT, 2, PR, PC), bf16),
            pltpu.VMEM((KEPT, 2, PR, PC), bf16),
            pltpu.VMEM((REPS, 2, PR, PC), bf16),
            pltpu.VMEM((REPS, 2, PR, PC), bf16),
            pltpu.VMEM((REPS, PR, PC), bf16),
            pltpu.VMEM((KEPT, PR, PC), bf16),
            pltpu.VMEM((KEPT, 2, PR, PC), bf16),
            pltpu.VMEM((slots, 3, PR, PC), bf16),
            pltpu.VMEM((slots, 3, PR, PC), bf16),
            pltpu.SemaphoreType.DMA((7,)),
            pltpu.SemaphoreType.DMA((6,)),
            pltpu.SemaphoreType.DMA((6,)),
            pltpu.SemaphoreType.DMA((3 * PARTS,)),
            pltpu.SemaphoreType.DMA((18 * PARTS,)),
            pltpu.SemaphoreType.DMA((18 * PARTS,)),
        ],
        compiler_params=pltpu.CompilerParams(
            collective_id=0, has_side_effects=True, vmem_limit_bytes=40 * 1024 * 1024
        ),
        cost_estimate=pl.CostEstimate(flops=12 * W**3, bytes_accessed=6 << 20, transcendentals=0),
        name="soap_step",
    )(idx, *operands)
    return tuple(
        pl.pallas_call(
            store_kernel,
            out_shape=outs,
            in_specs=[pl.BlockSpec(memory_space=pl.ANY)] * 5,
            out_specs=[hbm] * 5,
            scratch_shapes=[pltpu.SemaphoreType.DMA((12,))],
            compiler_params=pltpu.CompilerParams(vmem_limit_bytes=4 * 1024 * 1024),
            cost_estimate=pl.CostEstimate(flops=0, bytes_accessed=5 << 20, transcendentals=0),
            name="store",
        )(*results)
    )


def solution(mesh):
    rows = P("shard", "rep", None)
    return jax.shard_map(
        body,
        mesh=mesh,
        in_specs=(P("shard", None), P(), rows, rows, rows, rows, rows, rows),
        out_specs=(P("shard", None), rows, rows, rows, rows),
        check_vma=False,
    )
```

```python
import functools

import jax
import jax.numpy as jnp
from jax import lax
from jax.experimental import pallas as pl
from jax.experimental.pallas import tpu as pltpu
from jax.sharding import PartitionSpec as P

CAP = 2
BETA_ONE = 0.9
BETA_TWO = 0.95
EPSILON = 1e-08

YS = 8
ZS = 4
REPS = YS * ZS
SHARDS = 16
KEPT = 16
W = 256
PR, PC = 16, 128
PARTS = 4
FAR_Y = (4, 3, 5, 2, 6, 1, 7, 0)
FAR_Z = (2, 1, 3, 0)
MESH = pl.DeviceIdType.MESH


def routing(owner, here):
    flat = owner.T.reshape(-1)
    place = jnp.arange(flat.shape[0], dtype=jnp.int32)
    ident = place % owner.shape[0] * owner.shape[1] + place // owner.shape[0]
    source = ident // KEPT
    same = (flat[:, None] == flat[None, :]) & (ident[None, :] < ident[:, None])
    rank = jnp.sum(same.astype(jnp.int32), axis=1)
    pair = jnp.sum((same & (source[:, None] == source[None, :])).astype(jnp.int32), axis=1)
    local = jnp.arange(KEPT, dtype=jnp.int32)
    slots = jnp.arange(SHARDS * CAP, dtype=jnp.int32)
    mine = (ident[None, :] == here * KEPT + local[:, None]).astype(jnp.int32)
    dest = jnp.sum(mine * (flat * CAP + pair)[None, :], axis=1)
    owned = ((flat == here)[None, :] & (rank[None, :] == local[:, None])).astype(jnp.int32)
    recv = jnp.sum(owned * (source * CAP + pair)[None, :], axis=1)
    send_pick = jnp.sum((dest[None, :] == slots[:, None]).astype(jnp.int32) * local[None, :], axis=1)
    back_pick = jnp.sum((recv[None, :] == slots[:, None]).astype(jnp.int32) * local[None, :], axis=1)
    return jnp.concatenate([send_pick, recv, back_pick, dest])


def fold(x):
    x = x.astype(jnp.float32)
    return jnp.concatenate([x[:, :, :PC], x[:, :, PC:]], axis=1).astype(jnp.bfloat16)


def unfold(x):
    x = x.astype(jnp.float32)
    return jnp.concatenate([x[:, :8, :], x[:, 8:, :]], axis=2)


def nn(a, b):
    return lax.dot_general(a, b, (((1,), (0,)), ((), ())), preferred_element_type=jnp.float32)


def nt(a, b):
    return lax.dot_general(a, b, (((1,), (1,)), ((), ())), preferred_element_type=jnp.float32)


def tn(a, b):
    return lax.dot_general(a, b, (((0,), (0,)), ((), ())), preferred_element_type=jnp.float32)


def wait_bytes(ref, sem):
    pltpu.make_async_copy(ref, ref, sem).wait()


def kernel(
    idx, left_h, right_h, avg_h, avg_sq_h, grad, left_gram_h, right_gram_h,
    update, new_avg, new_avg_sq, new_left, new_right,
    left, right, avg, avg_sq, whole, left_gram, right_gram,
    folded, bases_out, moments_out, bases_in, moments_in, bases_row, moments_row, bases, moments,
    rsend, rbuf, grams, tsend, trecv,
    load_sem, send_sem, recv_sem, z_send, ag_send, ag_recv,
):
    r = lax.axis_index("rep")
    s = lax.axis_index("shard")
    y, z = r // ZS, r % ZS
    z_half, z_odd = z // 2, z % 2
    p0 = (y + s) % 2
    is_hub = z_odd == p0

    def wrap(v, n):
        return jnp.where(v >= n, v - n, v)

    ys = [wrap(y + t, YS) for t in range(YS)]
    zs = [wrap(z + t, ZS) for t in range(ZS)]
    z_low, x, core = s // 8, s % 8 // 2, s % 2
    xs = [wrap(x + t, 4) for t in range(4)]
    ss = [
        (1 - z_low if a else z_low) * 8 + xs[b] * 2 + (1 - core if c else core)
        for a, b, c in (
            (1, 2, 1), (1, 2, 0), (0, 2, 1), (0, 2, 0), (1, 1, 1), (1, 1, 0), (1, 3, 1), (1, 3, 0),
            (0, 1, 1), (0, 1, 0), (0, 3, 1), (0, 3, 0), (1, 0, 1), (1, 0, 0), (0, 0, 1),
        )
    ]

    def to(rep):
        return dict(device_id={"rep": rep}, device_id_type=MESH)

    def over(shard):
        return dict(device_id={"shard": shard}, device_id_type=MESH)

    loads = [
        pltpu.make_async_copy(src, dst, load_sem.at[n])
        for n, (src, dst) in enumerate(
            [(left_h, left), (right_h, right), (avg_h, avg), (avg_sq_h, avg_sq),
             (grad, whole), (left_gram_h, left_gram), (right_gram_h, right_gram)]
        )
    ]
    for copy in loads[:4]:
        copy.start()

    barrier = pltpu.get_barrier_semaphore()
    for peer in ss:
        pl.semaphore_signal(barrier, inc=1, **over(peer))

    @pl.when(is_hub)
    def _():
        for t in FAR_Y:
            for v in FAR_Z:
                if t or v:
                    pl.semaphore_signal(barrier, inc=1, **to(ys[t] * ZS + zs[v]))

    for n, ref in enumerate((left, right, avg, avg_sq)):
        loads[n].wait()
        folded[:, n] = fold(ref[...])
    for n in range(SHARDS * CAP):
        block = folded[idx[SHARDS * CAP + KEPT + n]]
        bases_out[n] = block[:2]
        moments_out[n] = block[2:]
    pl.semaphore_wait(barrier, jnp.where(is_hub, SHARDS - 1 + KEPT - 1, SHARDS - 1 + KEPT))

    mine = pl.ds(s * CAP, CAP)

    def exchange(src, dst, n):
        pltpu.make_async_copy(src.at[mine], dst.at[mine], recv_sem.at[n]).start()
        for peer in ss:
            pltpu.make_async_remote_copy(
                src.at[pl.ds(peer * CAP, CAP)], dst.at[mine], send_sem.at[n], recv_sem.at[n], **over(peer)
            ).start()

    exchange(bases_out, bases_in, 0)
    exchange(moments_out, moments_in, 1)
    for copy in loads[4:]:
        copy.start()

    def to_hub(src, dst, n):
        for t in FAR_Y:
            p = p0 if t % 2 == 0 else 1 - p0
            for b in (1 - z_half, z_half):
                block, h = 2 * ys[t] + b, ys[t] * ZS + 2 * b + p

                def remote(block=block, h=h):
                    pltpu.make_async_remote_copy(
                        src.at[block], dst.at[r], send_sem.at[n], recv_sem.at[n], **to(h)
                    ).start()

                if t == 0:
                    pl.when(h != r)(remote)

                    @pl.when(h == r)
                    def _(block=block):
                        pltpu.make_async_copy(src.at[block], dst.at[r], recv_sem.at[n]).start()
                else:
                    remote()

    for n, (got, row, out) in enumerate(
        ((bases_in, bases_row, bases), (moments_in, moments_row, moments))
    ):
        wait_bytes(got, recv_sem.at[n])
        for b in range(KEPT):
            row[b] = got[idx[2 * SHARDS * CAP + KEPT + b]]
        to_hub(row, out, 2 + n)

    block_me = 2 * y + z_half
    row_of = [pl.multiple_of(ys[t] // 4 * W, W) for t in range(YS)]
    col_of = [pl.multiple_of(ys[t] % 4 * (2 * W), W) for t in range(YS)]

    @pl.when(is_hub)
    def _():
        loads[4].wait()
        here = (pl.ds(row_of[0], W), pl.ds(pl.multiple_of(col_of[0] + z_half * W, W), W))
        g = whole[here]
        wait_bytes(bases, recv_sem.at[2])
        lb = unfold(bases[:, 0]).reshape(W, W).astype(jnp.bfloat16)
        rb = unfold(bases[:, 1]).reshape(W, W).astype(jnp.bfloat16)
        half = nn(lb, g).astype(jnp.bfloat16)
        turned = nn(half, rb)
        wait_bytes(moments, recv_sem.at[3])
        m0 = unfold(moments[:, 0]).reshape(W, W)
        v0 = unfold(moments[:, 1]).reshape(W, W)
        first = BETA_ONE * m0 + (1.0 - BETA_ONE) * turned
        second = BETA_TWO * v0 + (1.0 - BETA_TWO) * turned * turned
        scaled = (first / (jnp.sqrt(second) + EPSILON)).astype(jnp.bfloat16)
        back = nt(scaled, rb).astype(jnp.bfloat16)
        update[here] = tn(lb, back).astype(jnp.bfloat16)
        rsend[...] = fold(turned.reshape(REPS, 8, W))

    ups = (ys[1] * ZS + z, ys[7] * ZS + z)
    z_pair = 2 * z_half + 1 - z_odd
    z_next = jnp.where(z_odd == 1, zs[1], zs[3])
    pending = []
    names = {}

    def region(t, bit, rows):
        return update.at[
            pl.ds(pl.multiple_of(row_of[t] + rows[0], 16), rows[1] - rows[0]),
            pl.ds(pl.multiple_of(col_of[t] + bit * W, W), W),
        ]

    def push(ref, peer, key):
        n = names.setdefault(key, len(names))
        copy = pltpu.make_async_remote_copy(ref, ref, ag_send.at[n], ag_recv.at[n], **to(peer))
        copy.start()
        return copy

    def pull(ref, key):
        wait_bytes(ref, ag_recv.at[names[key]])

    bits = (z_half, 1 - z_half)
    parts = [(n * W // PARTS, (n + 1) * W // PARTS) for n in range(PARTS)]

    @pl.when(is_hub)
    def _():
        for m, rows in enumerate(parts):
            ref = region(0, bits[0], rows)
            for n, (c, peer) in enumerate(((1, zs[2]), (1, z_next), (0, z_pair))):
                key = names.setdefault(("z", c, m), len(names))
                pltpu.make_async_remote_copy(
                    ref, ref, z_send.at[3 * m + n], ag_recv.at[key], **to(y * ZS + peer)
                ).start()

    def y_rows(m, d, way):
        lo, hi = parts[m]
        if d < YS // 2:
            return lo, hi
        mid = (lo + hi) // 2
        return (lo, mid) if way == 0 else (mid, hi)

    def far(d, way):
        return (-d if way == 0 else d) % YS

    def y_push(c, m, d, way):
        ref = region(far(d - 1, way), bits[c], y_rows(m, d, way))
        pending.append(push(ref, ups[way], ("y", c, m, d, way)))

    def z_step(c, m):
        ref = region(0, bits[c], parts[m])
        if c == 0:
            pl.when(jnp.logical_not(is_hub))(lambda: pull(ref, ("z", c, m)))
        else:
            pull(ref, ("z", c, m))
        for way in range(2):
            y_push(c, m, 1, way)

    def y_step(c, m, d):
        for way in range(2):
            pull(region(far(d, way), bits[c], y_rows(m, d, way)), ("y", c, m, d, way))
            if d < YS // 2:
                y_push(c, m, d + 1, way)

    strip_at = pl.multiple_of(PR * (2 * y + z_half), PR)
    picks = (
        lax.broadcasted_iota(jnp.int32, (PR, W), 1)
        == lax.broadcasted_iota(jnp.int32, (PR, W), 0) + strip_at
    ).astype(jnp.float32).astype(jnp.bfloat16)

    def gram_rows(blocks):
        for b in blocks:
            i, j = b // 8, b % 8
            g = whole[i * W : (i + 1) * W, j * W : (j + 1) * W]
            strip = whole[pl.ds(i * W + strip_at, PR), j * W : (j + 1) * W]
            both = nt(jnp.concatenate([strip, picks], axis=0), g)
            wide = nn(both[PR:].astype(jnp.bfloat16), g)
            for n, v in enumerate((both[:PR], wide)):
                v = jnp.where(z_odd == 1, v[8:], v[:8])
                grams[b, n] = jnp.concatenate([v[:, :PC], v[:, PC:]], axis=0).astype(jnp.bfloat16)

    def side(n):
        if n == 0:

            @pl.when(jnp.logical_not(is_hub))
            def _():
                loads[4].wait()

        if n < YS // 2:

            @pl.when(is_hub)
            def _():
                for t in FAR_Y[2 * n : 2 * n + 2]:
                    for v in FAR_Z:
                        q = ys[t] * ZS + zs[v]
                        if t or v:
                            pltpu.make_async_remote_copy(
                                rsend.at[q], rbuf.at[block_me], send_sem.at[4], recv_sem.at[4], **to(q)
                            ).start()
                        else:
                            pltpu.make_async_copy(rsend.at[r], rbuf.at[block_me], recv_sem.at[4]).start()

        if n < KEPT // 2:
            gram_rows((2 * n, 2 * n + 1))
        elif n == KEPT // 2:
            wait_bytes(rbuf, recv_sem.at[4])
            for m in range(SHARDS * CAP):
                b = idx[m]
                tsend[m, 0] = rbuf[b]
                tsend[m, 1:] = grams[b]
            exchange(tsend, trecv, 5)

    def own_rows():
        wait_bytes(trecv, recv_sem.at[5])
        for copy in loads[5:]:
            copy.wait()
        for n in range(KEPT):
            turned, gl, gr = unfold(trecv[idx[SHARDS * CAP + n]])
            new_avg[n] = (BETA_ONE * avg[n].astype(jnp.float32) + (1.0 - BETA_ONE) * turned).astype(jnp.bfloat16)
            new_avg_sq[n] = BETA_TWO * avg_sq[n] + (1.0 - BETA_TWO) * turned * turned
            new_left[n] = BETA_TWO * left_gram[n] + (1.0 - BETA_TWO) * gl
            new_right[n] = BETA_TWO * right_gram[n] + (1.0 - BETA_TWO) * gr

    order = [(z_step, 0, m) for m in range(PARTS)]
    for m in range(PARTS):
        order += [(z_step, 1, m), (y_step, 0, m, 1)]
    order += [(y_step, 1, m, 1) for m in range(PARTS)]
    for d in (2, 3, 4):
        order += [(y_step, c, m, d) for c in range(2) for m in range(PARTS)]
    count = 0
    for step, *args in order[:-2]:
        step(*args)
        if count <= KEPT // 2:
            side(count)
        count += 1
        if count == len(order) - 4:
            own_rows()

    for copy in pending:
        copy.wait_send()
    for n, ref in ((0, bases_out), (1, moments_out), (5, tsend)):
        wait_bytes(ref.at[pl.ds(0, CAP * (SHARDS - 1))], send_sem.at[n])

    @pl.when(is_hub)
    def _():
        wait_bytes(bases_row.at[pl.ds(0, KEPT - 1)], send_sem.at[2])
        wait_bytes(moments_row.at[pl.ds(0, KEPT - 1)], send_sem.at[3])
        wait_bytes(rsend.at[pl.ds(0, REPS - 1)], send_sem.at[4])
        for n in range(3 * PARTS):
            wait_bytes(region(0, bits[0], parts[n // 3]), z_send.at[n])

    @pl.when(jnp.logical_not(is_hub))
    def _():
        wait_bytes(bases_row, send_sem.at[2])
        wait_bytes(moments_row, send_sem.at[3])

    for step, *args in order[-2:]:
        step(*args)


def store_kernel(*refs):
    count = len(refs) // 2
    sems = refs[-1]
    copies = []
    for n in range(count):
        src, dst = refs[n], refs[count + n]
        parts = 8 if n == 0 else 1
        size = src.shape[0] // parts
        for p in range(parts):
            rows = pl.ds(p * size, size)
            copies.append(pltpu.make_async_copy(src.at[rows], dst.at[rows], sems.at[len(copies)]))
    for copy in copies:
        copy.start()
    for copy in copies:
        copy.wait()


def body(grad, owner, left_basis, right_basis, avg, avg_sq, left_gram, right_gram):
    here = lax.axis_index("shard")
    idx = routing(owner, here)
    vmem = pl.BlockSpec(memory_space=pltpu.VMEM)
    hbm = pl.BlockSpec(memory_space=pltpu.HBM)
    bf16, f32 = jnp.bfloat16, jnp.float32
    slots = SHARDS * CAP
    rows = (KEPT, 8, W)
    outs = [jax.ShapeDtypeStruct(x.shape, x.dtype) for x in (grad, avg, avg_sq, left_gram, right_gram)]
    operands = [
        pltpu.with_memory_space_constraint(x, pltpu.HBM)
        for x in (left_basis, right_basis, avg, avg_sq, grad, left_gram, right_gram)
    ]
    results = pl.pallas_call(
        kernel,
        out_shape=outs,
        in_specs=[pl.BlockSpec(memory_space=pltpu.SMEM)] + [hbm] * 7,
        out_specs=[vmem] * 5,
        scratch_shapes=[
            pltpu.VMEM(rows, bf16),
            pltpu.VMEM(rows, bf16),
            pltpu.VMEM(rows, bf16),
            pltpu.VMEM(rows, f32),
            pltpu.VMEM(grad.shape, bf16),
            pltpu.VMEM(rows, f32),
            pltpu.VMEM(rows, f32),
            pltpu.VMEM((KEPT, 4, PR, PC), bf16),
            pltpu.VMEM((slots, 2, PR, PC), bf16),
            pltpu.VMEM((slots, 2, PR, PC), bf16),
            pltpu.VMEM((slots, 2, PR, PC), bf16),
            pltpu.VMEM((slots, 2, PR, PC), bf16),
            pltpu.VMEM((KEPT, 2, PR, PC), bf16),
            pltpu.VMEM((KEPT, 2, PR, PC), bf16),
            pltpu.VMEM((REPS, 2, PR, PC), bf16),
            pltpu.VMEM((REPS, 2, PR, PC), bf16),
            pltpu.VMEM((REPS, PR, PC), bf16),
            pltpu.VMEM((KEPT, PR, PC), bf16),
            pltpu.VMEM((KEPT, 2, PR, PC), bf16),
            pltpu.VMEM((slots, 3, PR, PC), bf16),
            pltpu.VMEM((slots, 3, PR, PC), bf16),
            pltpu.SemaphoreType.DMA((7,)),
            pltpu.SemaphoreType.DMA((6,)),
            pltpu.SemaphoreType.DMA((6,)),
            pltpu.SemaphoreType.DMA((3 * PARTS,)),
            pltpu.SemaphoreType.DMA((18 * PARTS,)),
            pltpu.SemaphoreType.DMA((18 * PARTS,)),
        ],
        compiler_params=pltpu.CompilerParams(
            collective_id=0, has_side_effects=True, vmem_limit_bytes=40 * 1024 * 1024
        ),
        cost_estimate=pl.CostEstimate(flops=12 * W**3, bytes_accessed=6 << 20, transcendentals=0),
        name="soap_step",
    )(idx, *operands)
    return tuple(
        pl.pallas_call(
            store_kernel,
            out_shape=outs,
            in_specs=[pl.BlockSpec(memory_space=pl.ANY)] * 5,
            out_specs=[hbm] * 5,
            scratch_shapes=[pltpu.SemaphoreType.DMA((12,))],
            compiler_params=pltpu.CompilerParams(vmem_limit_bytes=4 * 1024 * 1024),
            cost_estimate=pl.CostEstimate(flops=0, bytes_accessed=5 << 20, transcendentals=0),
            name="store",
        )(*results)
    )


def solution(mesh):
    rows = P("shard", "rep", None)
    return jax.shard_map(
        body,
        mesh=mesh,
        in_specs=(P("shard", None), P(), rows, rows, rows, rows, rows, rows),
        out_specs=(P("shard", None), rows, rows, rows, rows),
        check_vma=False,
    )
```

```python
import functools

import jax
import jax.numpy as jnp
from jax import lax
from jax.experimental import pallas as pl
from jax.experimental.pallas import tpu as pltpu
from jax.sharding import PartitionSpec as P

CAP = 2
BETA_ONE = 0.9
BETA_TWO = 0.95
EPSILON = 1e-08

YS = 8
ZS = 4
REPS = YS * ZS
SHARDS = 16
KEPT = 16
W = 256
PR, PC = 16, 128
PARTS = 2
FAR_Y = (4, 3, 5, 2, 6, 1, 7, 0)
FAR_Z = (2, 1, 3, 0)
MESH = pl.DeviceIdType.MESH


def routing(owner_t, here):
    i32, f32 = jnp.int32, jnp.float32
    count = owner_t.shape[0] * owner_t.shape[1]
    cols, rows = owner_t.shape
    square = lax.broadcasted_iota(i32, (rows, rows), 0) == lax.broadcasted_iota(i32, (rows, rows), 1)

    def total(mask, value, axis):
        return jnp.sum(jnp.where(mask, value, 0).astype(f32), axis=axis, keepdims=True).astype(i32)

    def numbers(shape, axis):
        at = lax.broadcasted_iota(i32, shape, axis)
        return at % rows * cols + at // rows, at % rows * cols // KEPT

    flat = jnp.concatenate([total(square, owner_t[j : j + 1, :], 1) for j in range(cols)], axis=0)
    ident, source = numbers((count, 1), 0)
    ident_r, source_r = numbers((1, count), 1)
    diagonal = ident == ident_r
    flat_r = total(diagonal, flat, 0)
    same = (flat == flat_r) & (ident_r < ident)
    rank = total(same, 1, 1)
    pair = total(same & (source == source_r), 1, 1)
    to_slot, from_slot = flat * CAP + pair, source * CAP + pair
    lane = lax.broadcasted_iota(i32, (1, 128), 1)
    slots = SHARDS * CAP
    owned = flat == here
    picked = jnp.where(
        lane < slots,
        jnp.where((source == here) & (to_slot == lane), ident - here * KEPT, 0),
        jnp.where(
            lane < slots + KEPT,
            jnp.where(owned & (rank == lane - slots), from_slot, 0),
            jnp.where(
                lane < 2 * slots + KEPT,
                jnp.where(owned & (from_slot == lane - slots - KEPT), rank, 0),
                jnp.where(ident == here * KEPT + lane - 2 * slots - KEPT, to_slot, 0),
            ),
        ),
    )
    row = jnp.sum(picked.astype(f32), axis=0, keepdims=True).astype(i32)
    of_slots = ((lane >= slots) & (lane < slots + KEPT)) | (lane >= 2 * slots + KEPT)
    row = jnp.maximum(jnp.minimum(row, jnp.where(of_slots, slots - 1, KEPT - 1)), 0)
    return jnp.broadcast_to(row, (8, 128))


def fold(x):
    x = x.astype(jnp.float32)
    return jnp.concatenate([x[:, :, :PC], x[:, :, PC:]], axis=1).astype(jnp.bfloat16)


def unfold(x):
    x = x.astype(jnp.float32)
    return jnp.concatenate([x[:, :8, :], x[:, 8:, :]], axis=2)


def nn(a, b):
    return lax.dot_general(a, b, (((1,), (0,)), ((), ())), preferred_element_type=jnp.float32)


def nt(a, b):
    return lax.dot_general(a, b, (((1,), (1,)), ((), ())), preferred_element_type=jnp.float32)


def tn(a, b):
    return lax.dot_general(a, b, (((0,), (0,)), ((), ())), preferred_element_type=jnp.float32)


def wait_bytes(ref, sem):
    pltpu.make_async_copy(ref, ref, sem).wait()


def kernel(
    owner_h, left_h, right_h, avg_h, avg_sq_h, grad, left_gram_h, right_gram_h,
    update, new_avg, new_avg_sq, new_left, new_right,
    owner, table_v, table, left, right, avg, avg_sq, whole, left_gram, right_gram,
    folded, bases_out, moments_out, bases_in, moments_in, bases_row, moments_row, bases, moments,
    rsend, rbuf, grams, tsend, trecv,
    load_sem, table_sem, send_sem, recv_sem, z_send, ag_send, ag_recv,
):
    r = lax.axis_index("rep")
    s = lax.axis_index("shard")
    y, z = r // ZS, r % ZS
    z_half, z_odd = z // 2, z % 2
    p0 = (y + s) % 2
    is_hub = z_odd == p0

    def wrap(v, n):
        return jnp.where(v >= n, v - n, v)

    ys = [wrap(y + t, YS) for t in range(YS)]
    zs = [wrap(z + t, ZS) for t in range(ZS)]
    z_low, x, core = s // 8, s % 8 // 2, s % 2
    xs = [wrap(x + t, 4) for t in range(4)]
    ss = [
        (1 - z_low if a else z_low) * 8 + xs[b] * 2 + (1 - core if c else core)
        for a, b, c in (
            (1, 2, 1), (1, 2, 0), (0, 2, 1), (0, 2, 0), (1, 1, 1), (1, 1, 0), (1, 3, 1), (1, 3, 0),
            (0, 1, 1), (0, 1, 0), (0, 3, 1), (0, 3, 0), (1, 0, 1), (1, 0, 0), (0, 0, 1),
        )
    ]

    def to(rep):
        return dict(device_id={"rep": rep}, device_id_type=MESH)

    def over(shard):
        return dict(device_id={"shard": shard}, device_id_type=MESH)

    loads = [
        pltpu.make_async_copy(src, dst, load_sem.at[n])
        for n, (src, dst) in enumerate(
            [(left_h, left), (right_h, right), (avg_h, avg), (avg_sq_h, avg_sq),
             (grad, whole), (left_gram_h, left_gram), (right_gram_h, right_gram), (owner_h, owner)]
        )
    ]
    for copy in (loads[7], *loads[:4]):
        copy.start()

    def idx(n):
        return table[0, n]

    barrier = pltpu.get_barrier_semaphore()
    for peer in ss:
        pl.semaphore_signal(barrier, inc=1, **over(peer))

    @pl.when(is_hub)
    def _():
        for t in FAR_Y:
            for v in FAR_Z:
                if t or v:
                    pl.semaphore_signal(barrier, inc=1, **to(ys[t] * ZS + zs[v]))

    loads[7].wait()
    table_v[...] = routing(owner[...], s)
    pltpu.make_async_copy(table_v, table, table_sem).start()

    def pack(first, refs, out):
        for n, ref in enumerate(refs):
            loads[first + n].wait()
            folded[:, n] = fold(ref[...])
        if first == 0:
            pltpu.make_async_copy(table_v, table, table_sem).wait()
        for n in range(SHARDS * CAP):
            out[n] = folded[idx(SHARDS * CAP + KEPT + n)]

    pack(0, (left, right), bases_out)
    pl.semaphore_wait(barrier, jnp.where(is_hub, SHARDS - 1 + KEPT - 1, SHARDS - 1 + KEPT))

    mine = pl.ds(s * CAP, CAP)

    def exchange(src, dst, n):
        pltpu.make_async_copy(src.at[mine], dst.at[mine], recv_sem.at[n]).start()
        for peer in ss:
            pltpu.make_async_remote_copy(
                src.at[pl.ds(peer * CAP, CAP)], dst.at[mine], send_sem.at[n], recv_sem.at[n], **over(peer)
            ).start()

    exchange(bases_out, bases_in, 0)
    pack(2, (avg, avg_sq), moments_out)
    exchange(moments_out, moments_in, 1)
    for copy in loads[4:7]:
        copy.start()

    def to_hub(src, dst, n):
        for t in FAR_Y:
            p = p0 if t % 2 == 0 else 1 - p0
            for b in (1 - z_half, z_half):
                block, h = 2 * ys[t] + b, ys[t] * ZS + 2 * b + p

                def remote(block=block, h=h):
                    pltpu.make_async_remote_copy(
                        src.at[block], dst.at[r], send_sem.at[n], recv_sem.at[n], **to(h)
                    ).start()

                if t == 0:
                    pl.when(h != r)(remote)

                    @pl.when(h == r)
                    def _(block=block):
                        pltpu.make_async_copy(src.at[block], dst.at[r], recv_sem.at[n]).start()
                else:
                    remote()

    for n, (got, row, out) in enumerate(
        ((bases_in, bases_row, bases), (moments_in, moments_row, moments))
    ):
        wait_bytes(got, recv_sem.at[n])
        for b in range(KEPT):
            row[b] = got[idx(2 * SHARDS * CAP + KEPT + b)]
        to_hub(row, out, 2 + n)

    block_me = 2 * y + z_half

    @pl.when(is_hub)
    def _():
        loads[4].wait()
        g = whole[
            pl.ds(pl.multiple_of(y // 4 * W, W), W),
            pl.ds(pl.multiple_of(y % 4 * (2 * W) + z_half * W, W), W),
        ]
        wait_bytes(bases, recv_sem.at[2])
        lb = unfold(bases[:, 0]).reshape(W, W).astype(jnp.bfloat16)
        rb = unfold(bases[:, 1]).reshape(W, W).astype(jnp.bfloat16)
        half = nn(lb, g).astype(jnp.bfloat16)
        turned = nn(half, rb)
        wait_bytes(moments, recv_sem.at[3])
        m0 = unfold(moments[:, 0]).reshape(W, W)
        v0 = unfold(moments[:, 1]).reshape(W, W)
        first = BETA_ONE * m0 + (1.0 - BETA_ONE) * turned
        second = BETA_TWO * v0 + (1.0 - BETA_TWO) * turned * turned
        scaled = (first / (jnp.sqrt(second) + EPSILON)).astype(jnp.bfloat16)
        back = nt(scaled, rb).astype(jnp.bfloat16)
        update[block_me] = tn(lb, back).astype(jnp.bfloat16)
        rsend[...] = fold(turned.reshape(REPS, 8, W))

    ups = (ys[1] * ZS + z, ys[7] * ZS + z)
    z_pair = 2 * z_half + 1 - z_odd
    z_next = jnp.where(z_odd == 1, zs[1], zs[3])
    pending = []
    names = {}

    def region(t, bit, rows):
        return update.at[2 * ys[t] + bit, pl.ds(rows[0], rows[1] - rows[0])]

    def push(ref, peer, key):
        n = names.setdefault(key, len(names))
        copy = pltpu.make_async_remote_copy(ref, ref, ag_send.at[n], ag_recv.at[n], **to(peer))
        copy.start()
        return copy

    def pull(ref, key):
        wait_bytes(ref, ag_recv.at[names[key]])

    bits = (z_half, 1 - z_half)
    parts = [(n * W // PARTS, (n + 1) * W // PARTS) for n in range(PARTS)]

    @pl.when(is_hub)
    def _():
        for m, rows in enumerate(parts):
            ref = region(0, bits[0], rows)
            for n, (c, peer) in enumerate(((1, zs[2]), (1, z_next), (0, z_pair))):
                key = names.setdefault(("z", c, m), len(names))
                pltpu.make_async_remote_copy(
                    ref, ref, z_send.at[3 * m + n], ag_recv.at[key], **to(y * ZS + peer)
                ).start()

    def y_rows(m, d, way):
        lo, hi = parts[m]
        if d < YS // 2:
            return lo, hi
        mid = (lo + hi) // 2
        return (lo, mid) if way == 0 else (mid, hi)

    def far(d, way):
        return (-d if way == 0 else d) % YS

    def y_push(c, m, d, way):
        ref = region(far(d - 1, way), bits[c], y_rows(m, d, way))
        pending.append(push(ref, ups[way], ("y", c, m, d, way)))

    def z_step(c, m):
        ref = region(0, bits[c], parts[m])
        if c == 0:
            pl.when(jnp.logical_not(is_hub))(lambda: pull(ref, ("z", c, m)))
        else:
            pull(ref, ("z", c, m))
        for way in range(2):
            y_push(c, m, 1, way)

    def y_step(c, m, d):
        for way in range(2):
            pull(region(far(d, way), bits[c], y_rows(m, d, way)), ("y", c, m, d, way))
            if d < YS // 2:
                y_push(c, m, d + 1, way)

    strip_at = pl.multiple_of(PR * (2 * y + z_half), PR)
    picks = (
        lax.broadcasted_iota(jnp.int32, (PR, W), 1)
        == lax.broadcasted_iota(jnp.int32, (PR, W), 0) + strip_at
    ).astype(jnp.float32).astype(jnp.bfloat16)

    def gram_rows(blocks):
        for b in blocks:
            i, j = b // 8, b % 8
            g = whole[i * W : (i + 1) * W, j * W : (j + 1) * W]
            strip = whole[pl.ds(i * W + strip_at, PR), j * W : (j + 1) * W]
            both = nt(jnp.concatenate([strip, picks], axis=0), g)
            wide = nn(both[PR:].astype(jnp.bfloat16), g)
            for n, v in enumerate((both[:PR], wide)):
                v = jnp.where(z_odd == 1, v[8:], v[:8])
                grams[b, n] = jnp.concatenate([v[:, :PC], v[:, PC:]], axis=0).astype(jnp.bfloat16)

    def send_r(n):
        @pl.when(is_hub)
        def _():
            t = FAR_Y[n]
            for v in FAR_Z:
                q = ys[t] * ZS + zs[v]
                if t or v:
                    pltpu.make_async_remote_copy(
                        rsend.at[q], rbuf.at[block_me], send_sem.at[4], recv_sem.at[4], **to(q)
                    ).start()
                else:
                    pltpu.make_async_copy(rsend.at[r], rbuf.at[block_me], recv_sem.at[4]).start()

    def to_owners():
        wait_bytes(rbuf, recv_sem.at[4])
        for m in range(SHARDS * CAP):
            b = idx(m)
            tsend[m, 0] = rbuf[b]
            tsend[m, 1:] = grams[b]
        exchange(tsend, trecv, 5)

    def side(n):
        if n == 0:

            @pl.when(jnp.logical_not(is_hub))
            def _():
                loads[4].wait()

        if n < YS:
            send_r(n)
            gram_rows((2 * n, 2 * n + 1))
        elif n == YS:
            to_owners()

    def own_rows():
        wait_bytes(trecv, recv_sem.at[5])
        for copy in loads[5:7]:
            copy.wait()
        for n in range(KEPT):
            turned, gl, gr = unfold(trecv[idx(SHARDS * CAP + n)])
            new_avg[n] = (BETA_ONE * avg[n].astype(jnp.float32) + (1.0 - BETA_ONE) * turned).astype(jnp.bfloat16)
            new_avg_sq[n] = BETA_TWO * avg_sq[n] + (1.0 - BETA_TWO) * turned * turned
            new_left[n] = BETA_TWO * left_gram[n] + (1.0 - BETA_TWO) * gl
            new_right[n] = BETA_TWO * right_gram[n] + (1.0 - BETA_TWO) * gr

    order = [(z_step, 0, m) for m in range(PARTS)]
    for m in range(PARTS):
        order += [(z_step, 1, m), (y_step, 0, m, 1)]
    order += [(y_step, 1, m, 1) for m in range(PARTS)]
    for d in (2, 3, 4):
        order += [(y_step, c, m, d) for c in range(2) for m in range(PARTS)]
    first = 2 * PARTS - 1
    for count, (step, *args) in enumerate(order[:-2]):
        step(*args)
        if first <= count <= first + YS:
            side(count - first)
        if count == len(order) - 4:
            own_rows()

    for copy in pending:
        copy.wait_send()
    for n, ref in ((0, bases_out), (1, moments_out), (5, tsend)):
        wait_bytes(ref.at[pl.ds(0, CAP * (SHARDS - 1))], send_sem.at[n])

    @pl.when(is_hub)
    def _():
        wait_bytes(bases_row.at[pl.ds(0, KEPT - 1)], send_sem.at[2])
        wait_bytes(moments_row.at[pl.ds(0, KEPT - 1)], send_sem.at[3])
        wait_bytes(rsend.at[pl.ds(0, REPS - 1)], send_sem.at[4])
        for n in range(3 * PARTS):
            wait_bytes(region(0, bits[0], parts[n // 3]), z_send.at[n])

    @pl.when(jnp.logical_not(is_hub))
    def _():
        wait_bytes(bases_row, send_sem.at[2])
        wait_bytes(moments_row, send_sem.at[3])

    for step, *args in order[-2:]:
        step(*args)


def store_kernel(*refs):
    count = len(refs) // 2
    sems = refs[-1]
    copies = []
    for n in range(count):
        src, dst = refs[n], refs[count + n]
        if n == 0:
            for b in range(KEPT):
                i, j = b // 8, b % 8
                place = dst.at[i * W : (i + 1) * W, j * W : (j + 1) * W]
                copies.append(pltpu.make_async_copy(src.at[b], place, sems.at[len(copies)]))
        else:
            copies.append(pltpu.make_async_copy(src, dst, sems.at[len(copies)]))
    for copy in copies:
        copy.start()
    for copy in copies:
        copy.wait()


def body(grad, owner, left_basis, right_basis, avg, avg_sq, left_gram, right_gram):
    vmem = pl.BlockSpec(memory_space=pltpu.VMEM)
    hbm = pl.BlockSpec(memory_space=pltpu.HBM)
    bf16, f32 = jnp.bfloat16, jnp.float32
    slots = SHARDS * CAP
    rows = (KEPT, 8, W)
    outs = [jax.ShapeDtypeStruct(x.shape, x.dtype) for x in (grad, avg, avg_sq, left_gram, right_gram)]
    operands = [
        pltpu.with_memory_space_constraint(x, pltpu.HBM)
        for x in (owner.T, left_basis, right_basis, avg, avg_sq, grad, left_gram, right_gram)
    ]
    results = pl.pallas_call(
        kernel,
        out_shape=[jax.ShapeDtypeStruct((KEPT, W, W), bf16)] + outs[1:],
        in_specs=[hbm] * 8,
        out_specs=[vmem] * 5,
        scratch_shapes=[
            pltpu.VMEM(owner.shape[::-1], jnp.int32),
            pltpu.VMEM((8, 128), jnp.int32),
            pltpu.SMEM((8, 128), jnp.int32),
            pltpu.VMEM(rows, bf16),
            pltpu.VMEM(rows, bf16),
            pltpu.VMEM(rows, bf16),
            pltpu.VMEM(rows, f32),
            pltpu.VMEM(grad.shape, bf16),
            pltpu.VMEM(rows, f32),
            pltpu.VMEM(rows, f32),
            pltpu.VMEM((KEPT, 2, PR, PC), bf16),
            pltpu.VMEM((slots, 2, PR, PC), bf16),
            pltpu.VMEM((slots, 2, PR, PC), bf16),
            pltpu.VMEM((slots, 2, PR, PC), bf16),
            pltpu.VMEM((slots, 2, PR, PC), bf16),
            pltpu.VMEM((KEPT, 2, PR, PC), bf16),
            pltpu.VMEM((KEPT, 2, PR, PC), bf16),
            pltpu.VMEM((REPS, 2, PR, PC), bf16),
            pltpu.VMEM((REPS, 2, PR, PC), bf16),
            pltpu.VMEM((REPS, PR, PC), bf16),
            pltpu.VMEM((KEPT, PR, PC), bf16),
            pltpu.VMEM((KEPT, 2, PR, PC), bf16),
            pltpu.VMEM((slots, 3, PR, PC), bf16),
            pltpu.VMEM((slots, 3, PR, PC), bf16),
            pltpu.SemaphoreType.DMA((8,)),
            pltpu.SemaphoreType.DMA,
            pltpu.SemaphoreType.DMA((6,)),
            pltpu.SemaphoreType.DMA((6,)),
            pltpu.SemaphoreType.DMA((3 * PARTS,)),
            pltpu.SemaphoreType.DMA((18 * PARTS,)),
            pltpu.SemaphoreType.DMA((18 * PARTS,)),
        ],
        compiler_params=pltpu.CompilerParams(
            collective_id=0, has_side_effects=True, vmem_limit_bytes=40 * 1024 * 1024
        ),
        cost_estimate=pl.CostEstimate(flops=12 * W**3, bytes_accessed=6 << 20, transcendentals=0),
        name="soap_step",
    )(*operands)
    return tuple(
        pl.pallas_call(
            store_kernel,
            out_shape=outs,
            in_specs=[pl.BlockSpec(memory_space=pl.ANY)] * 5,
            out_specs=[hbm] * 5,
            scratch_shapes=[pltpu.SemaphoreType.DMA((KEPT + 4,))],
            compiler_params=pltpu.CompilerParams(vmem_limit_bytes=4 * 1024 * 1024),
            cost_estimate=pl.CostEstimate(flops=0, bytes_accessed=5 << 20, transcendentals=0),
            name="store",
        )(*results)
    )


def solution(mesh):
    rows = P("shard", "rep", None)
    return jax.shard_map(
        body,
        mesh=mesh,
        in_specs=(P("shard", None), P(), rows, rows, rows, rows, rows, rows),
        out_specs=(P("shard", None), rows, rows, rows, rows),
        check_vma=False,
    )
```

```python
import functools

import jax
import jax.numpy as jnp
from jax import lax
from jax.experimental import pallas as pl
from jax.experimental.pallas import tpu as pltpu
from jax.sharding import PartitionSpec as P

CAP = 2
BETA_ONE = 0.9
BETA_TWO = 0.95
EPSILON = 1e-08

YS = 8
ZS = 4
REPS = YS * ZS
SHARDS = 16
KEPT = 16
W = 256
PR, PC = 16, 128
PARTS = 2
FAR_Y = (4, 3, 5, 2, 6, 1, 7, 0)
FAR_Z = (2, 1, 3, 0)
MESH = pl.DeviceIdType.MESH


def routing(owner_t, here):
    i32, f32 = jnp.int32, jnp.float32
    count = owner_t.shape[0] * owner_t.shape[1]
    cols, rows = owner_t.shape
    square = lax.broadcasted_iota(i32, (rows, rows), 0) == lax.broadcasted_iota(i32, (rows, rows), 1)

    def total(mask, value, axis):
        return jnp.sum(jnp.where(mask, value, 0).astype(f32), axis=axis, keepdims=True).astype(i32)

    def numbers(shape, axis):
        at = lax.broadcasted_iota(i32, shape, axis)
        return at % rows * cols + at // rows, at % rows * cols // KEPT

    flat = jnp.concatenate([total(square, owner_t[j : j + 1, :], 1) for j in range(cols)], axis=0)
    ident, source = numbers((count, 1), 0)
    ident_r, source_r = numbers((1, count), 1)
    diagonal = ident == ident_r
    flat_r = total(diagonal, flat, 0)
    same = (flat == flat_r) & (ident_r < ident)
    rank = total(same, 1, 1)
    pair = total(same & (source == source_r), 1, 1)
    to_slot, from_slot = flat * CAP + pair, source * CAP + pair
    lane = lax.broadcasted_iota(i32, (1, 128), 1)
    slots = SHARDS * CAP
    owned = flat == here
    picked = jnp.where(
        lane < slots,
        jnp.where((source == here) & (to_slot == lane), ident - here * KEPT, 0),
        jnp.where(
            lane < slots + KEPT,
            jnp.where(owned & (rank == lane - slots), from_slot, 0),
            jnp.where(
                lane < 2 * slots + KEPT,
                jnp.where(owned & (from_slot == lane - slots - KEPT), rank, 0),
                jnp.where(ident == here * KEPT + lane - 2 * slots - KEPT, to_slot, 0),
            ),
        ),
    )
    row = jnp.sum(picked.astype(f32), axis=0, keepdims=True).astype(i32)
    of_slots = ((lane >= slots) & (lane < slots + KEPT)) | (lane >= 2 * slots + KEPT)
    row = jnp.maximum(jnp.minimum(row, jnp.where(of_slots, slots - 1, KEPT - 1)), 0)
    return jnp.broadcast_to(row, (8, 128))


def fold(x):
    x = x.astype(jnp.float32)
    return jnp.concatenate([x[:, :, :PC], x[:, :, PC:]], axis=1).astype(jnp.bfloat16)


def unfold(x):
    x = x.astype(jnp.float32)
    return jnp.concatenate([x[:, :8, :], x[:, 8:, :]], axis=2)


def nn(a, b):
    return lax.dot_general(a, b, (((1,), (0,)), ((), ())), preferred_element_type=jnp.float32)


def nt(a, b):
    return lax.dot_general(a, b, (((1,), (1,)), ((), ())), preferred_element_type=jnp.float32)


def tn(a, b):
    return lax.dot_general(a, b, (((0,), (0,)), ((), ())), preferred_element_type=jnp.float32)


def wait_bytes(ref, sem):
    pltpu.make_async_copy(ref, ref, sem).wait()


def kernel(
    owner_h, left_h, right_h, avg_h, avg_sq_h, grad, left_gram_h, right_gram_h,
    update, new_avg, new_avg_sq, new_left, new_right,
    owner, table_v, table, left, right, avg, avg_sq, whole, left_gram, right_gram,
    folded, bases_out, moments_out, bases_in, moments_in, bases_row, moments_row, bases, moments,
    rsend, rbuf, grams, tsend, trecv,
    load_sem, table_sem, send_sem, recv_sem, z_send, ag_send, ag_recv,
):
    r = lax.axis_index("rep")
    s = lax.axis_index("shard")
    y, z = r // ZS, r % ZS
    z_half, z_odd = z // 2, z % 2
    p0 = (y + s) % 2
    is_hub = z_odd == p0

    def wrap(v, n):
        return jnp.where(v >= n, v - n, v)

    ys = [wrap(y + t, YS) for t in range(YS)]
    zs = [wrap(z + t, ZS) for t in range(ZS)]
    z_low, x, core = s // 8, s % 8 // 2, s % 2
    xs = [wrap(x + t, 4) for t in range(4)]
    ss = [
        (1 - z_low if a else z_low) * 8 + xs[b] * 2 + (1 - core if c else core)
        for a, b, c in (
            (1, 2, 1), (1, 2, 0), (0, 2, 1), (0, 2, 0), (1, 1, 1), (1, 1, 0), (1, 3, 1), (1, 3, 0),
            (0, 1, 1), (0, 1, 0), (0, 3, 1), (0, 3, 0), (1, 0, 1), (1, 0, 0), (0, 0, 1),
        )
    ]

    def to(rep):
        return dict(device_id={"rep": rep}, device_id_type=MESH)

    def over(shard):
        return dict(device_id={"shard": shard}, device_id_type=MESH)

    loads = [
        pltpu.make_async_copy(src, dst, load_sem.at[n])
        for n, (src, dst) in enumerate(
            [(left_h, left), (right_h, right), (avg_h, avg), (avg_sq_h, avg_sq),
             (grad, whole), (left_gram_h, left_gram), (right_gram_h, right_gram), (owner_h, owner)]
        )
    ]
    for copy in (loads[7], *loads[:4]):
        copy.start()

    def idx(n):
        return table[0, n]

    barrier = pltpu.get_barrier_semaphore()
    for peer in ss:
        pl.semaphore_signal(barrier, inc=1, **over(peer))

    @pl.when(is_hub)
    def _():
        for t in FAR_Y:
            for v in FAR_Z:
                if t or v:
                    pl.semaphore_signal(barrier, inc=1, **to(ys[t] * ZS + zs[v]))

    loads[7].wait()
    table_v[...] = routing(owner[...], s)
    pltpu.make_async_copy(table_v, table, table_sem).start()

    def pack(first, refs, out):
        for n, ref in enumerate(refs):
            loads[first + n].wait()
            folded[:, n] = fold(ref[...])
        if first == 0:
            pltpu.make_async_copy(table_v, table, table_sem).wait()
        for n in range(SHARDS * CAP):
            out[n] = folded[idx(SHARDS * CAP + KEPT + n)]

    pack(0, (left, right), bases_out)
    pl.semaphore_wait(barrier, jnp.where(is_hub, SHARDS - 1 + KEPT - 1, SHARDS - 1 + KEPT))

    mine = pl.ds(s * CAP, CAP)

    def exchange(src, dst, n):
        pltpu.make_async_copy(src.at[mine], dst.at[mine], recv_sem.at[n]).start()
        for peer in ss:
            pltpu.make_async_remote_copy(
                src.at[pl.ds(peer * CAP, CAP)], dst.at[mine], send_sem.at[n], recv_sem.at[n], **over(peer)
            ).start()

    exchange(bases_out, bases_in, 0)
    pack(2, (avg, avg_sq), moments_out)
    exchange(moments_out, moments_in, 1)
    for copy in loads[4:7]:
        copy.start()

    strip_at = pl.multiple_of(PR * (2 * y + z_half), PR)
    picks = (
        lax.broadcasted_iota(jnp.int32, (PR, W), 1)
        == lax.broadcasted_iota(jnp.int32, (PR, W), 0) + strip_at
    ).astype(jnp.float32).astype(jnp.bfloat16)

    def gram_rows(blocks):
        for b in blocks:
            i, j = b // 8, b % 8
            g = whole[i * W : (i + 1) * W, j * W : (j + 1) * W]
            strip = whole[pl.ds(i * W + strip_at, PR), j * W : (j + 1) * W]
            both = nt(jnp.concatenate([strip, picks], axis=0), g)
            wide = nn(both[PR:].astype(jnp.bfloat16), g)
            for n, v in enumerate((both[:PR], wide)):
                v = jnp.where(z_odd == 1, v[8:], v[:8])
                grams[b, n] = jnp.concatenate([v[:, :PC], v[:, PC:]], axis=0).astype(jnp.bfloat16)

    def to_hub(src, dst, n):
        for t in FAR_Y:
            p = p0 if t % 2 == 0 else 1 - p0
            for b in (1 - z_half, z_half):
                block, h = 2 * ys[t] + b, ys[t] * ZS + 2 * b + p

                def remote(block=block, h=h):
                    pltpu.make_async_remote_copy(
                        src.at[block], dst.at[r], send_sem.at[n], recv_sem.at[n], **to(h)
                    ).start()

                if t == 0:
                    pl.when(h != r)(remote)

                    @pl.when(h == r)
                    def _(block=block):
                        pltpu.make_async_copy(src.at[block], dst.at[r], recv_sem.at[n]).start()
                else:
                    remote()

    loads[4].wait()
    gram_rows(range(0, 6))
    for n, (got, row, out) in enumerate(
        ((bases_in, bases_row, bases), (moments_in, moments_row, moments))
    ):
        wait_bytes(got, recv_sem.at[n])
        for b in range(KEPT):
            row[b] = got[idx(2 * SHARDS * CAP + KEPT + b)]
        to_hub(row, out, 2 + n)
        gram_rows(range(6, 10) if n == 0 else range(10, KEPT))

    block_me = 2 * y + z_half

    @pl.when(is_hub)
    def _():
        g = whole[
            pl.ds(pl.multiple_of(y // 4 * W, W), W),
            pl.ds(pl.multiple_of(y % 4 * (2 * W) + z_half * W, W), W),
        ]
        wait_bytes(bases, recv_sem.at[2])
        lb = unfold(bases[:, 0]).reshape(W, W).astype(jnp.bfloat16)
        rb = unfold(bases[:, 1]).reshape(W, W).astype(jnp.bfloat16)
        half = nn(lb, g).astype(jnp.bfloat16)
        turned = nn(half, rb)
        wait_bytes(moments, recv_sem.at[3])
        m0 = unfold(moments[:, 0]).reshape(W, W)
        v0 = unfold(moments[:, 1]).reshape(W, W)
        first = BETA_ONE * m0 + (1.0 - BETA_ONE) * turned
        second = BETA_TWO * v0 + (1.0 - BETA_TWO) * turned * turned
        scaled = (first / (jnp.sqrt(second) + EPSILON)).astype(jnp.bfloat16)
        back = nt(scaled, rb).astype(jnp.bfloat16)
        update[block_me] = tn(lb, back).astype(jnp.bfloat16)
        rsend[...] = fold(turned.reshape(REPS, 8, W))

    ups = (ys[1] * ZS + z, ys[7] * ZS + z)
    z_pair = 2 * z_half + 1 - z_odd
    z_next = jnp.where(z_odd == 1, zs[1], zs[3])
    pending = []
    names = {}

    def region(t, bit, rows):
        return update.at[2 * ys[t] + bit, pl.ds(rows[0], rows[1] - rows[0])]

    def push(ref, peer, key):
        n = names.setdefault(key, len(names))
        copy = pltpu.make_async_remote_copy(ref, ref, ag_send.at[n], ag_recv.at[n], **to(peer))
        copy.start()
        return copy

    def pull(ref, key):
        wait_bytes(ref, ag_recv.at[names[key]])

    bits = (z_half, 1 - z_half)
    parts = [(n * W // PARTS, (n + 1) * W // PARTS) for n in range(PARTS)]

    @pl.when(is_hub)
    def _():
        for m, rows in enumerate(parts):
            ref = region(0, bits[0], rows)
            for n, (c, peer) in enumerate(((1, zs[2]), (1, z_next), (0, z_pair))):
                key = names.setdefault(("z", c, m), len(names))
                pltpu.make_async_remote_copy(
                    ref, ref, z_send.at[3 * m + n], ag_recv.at[key], **to(y * ZS + peer)
                ).start()

    def y_rows(m, d, way):
        lo, hi = parts[m]
        if d < YS // 2:
            return lo, hi
        mid = (lo + hi) // 2
        return (lo, mid) if way == 0 else (mid, hi)

    def far(d, way):
        return (-d if way == 0 else d) % YS

    def y_push(c, m, d, way):
        ref = region(far(d - 1, way), bits[c], y_rows(m, d, way))
        pending.append(push(ref, ups[way], ("y", c, m, d, way)))

    def z_step(c, m):
        ref = region(0, bits[c], parts[m])
        if c == 0:
            pl.when(jnp.logical_not(is_hub))(lambda: pull(ref, ("z", c, m)))
        else:
            pull(ref, ("z", c, m))
        for way in range(2):
            y_push(c, m, 1, way)

    def y_step(c, m, d):
        for way in range(2):
            pull(region(far(d, way), bits[c], y_rows(m, d, way)), ("y", c, m, d, way))
            if d < YS // 2:
                y_push(c, m, d + 1, way)

    def send_r():
        @pl.when(is_hub)
        def _():
            for t in FAR_Y:
                for v in FAR_Z:
                    q = ys[t] * ZS + zs[v]
                    if t or v:
                        pltpu.make_async_remote_copy(
                            rsend.at[q], rbuf.at[block_me], send_sem.at[4], recv_sem.at[4], **to(q)
                        ).start()
                    else:
                        pltpu.make_async_copy(rsend.at[r], rbuf.at[block_me], recv_sem.at[4]).start()

    def to_owners():
        wait_bytes(rbuf, recv_sem.at[4])
        for m in range(SHARDS * CAP):
            b = idx(m)
            tsend[m, 0] = rbuf[b]
            tsend[m, 1:] = grams[b]
        exchange(tsend, trecv, 5)

    def own_rows():
        wait_bytes(trecv, recv_sem.at[5])
        for copy in loads[5:7]:
            copy.wait()
        for n in range(KEPT):
            turned, gl, gr = unfold(trecv[idx(SHARDS * CAP + n)])
            new_avg[n] = (BETA_ONE * avg[n].astype(jnp.float32) + (1.0 - BETA_ONE) * turned).astype(jnp.bfloat16)
            new_avg_sq[n] = BETA_TWO * avg_sq[n] + (1.0 - BETA_TWO) * turned * turned
            new_left[n] = BETA_TWO * left_gram[n] + (1.0 - BETA_TWO) * gl
            new_right[n] = BETA_TWO * right_gram[n] + (1.0 - BETA_TWO) * gr

    order = [(z_step, 0, m) for m in range(PARTS)]
    for m in range(PARTS):
        order += [(z_step, 1, m), (y_step, 0, m, 1)]
    order += [(y_step, 1, m, 1) for m in range(PARTS)]
    for d in (2, 3, 4):
        order += [(y_step, c, m, d) for c in range(2) for m in range(PARTS)]
    for count, (step, *args) in enumerate(order[:-2]):
        step(*args)
        if count == PARTS - 1:
            send_r()
        if count == 4 * PARTS:
            to_owners()
        if count == len(order) - 4:
            own_rows()

    for copy in pending:
        copy.wait_send()
    for n, ref in ((0, bases_out), (1, moments_out), (5, tsend)):
        wait_bytes(ref.at[pl.ds(0, CAP * (SHARDS - 1))], send_sem.at[n])

    @pl.when(is_hub)
    def _():
        wait_bytes(bases_row.at[pl.ds(0, KEPT - 1)], send_sem.at[2])
        wait_bytes(moments_row.at[pl.ds(0, KEPT - 1)], send_sem.at[3])
        wait_bytes(rsend.at[pl.ds(0, REPS - 1)], send_sem.at[4])
        for n in range(3 * PARTS):
            wait_bytes(region(0, bits[0], parts[n // 3]), z_send.at[n])

    @pl.when(jnp.logical_not(is_hub))
    def _():
        wait_bytes(bases_row, send_sem.at[2])
        wait_bytes(moments_row, send_sem.at[3])

    for step, *args in order[-2:]:
        step(*args)


def store_kernel(*refs):
    count = len(refs) // 2
    sems = refs[-1]
    copies = []
    for n in range(count):
        src, dst = refs[n], refs[count + n]
        if n == 0:
            for b in range(KEPT):
                i, j = b // 8, b % 8
                place = dst.at[i * W : (i + 1) * W, j * W : (j + 1) * W]
                copies.append(pltpu.make_async_copy(src.at[b], place, sems.at[len(copies)]))
        else:
            copies.append(pltpu.make_async_copy(src, dst, sems.at[len(copies)]))
    for copy in copies:
        copy.start()
    for copy in copies:
        copy.wait()


def body(grad, owner, left_basis, right_basis, avg, avg_sq, left_gram, right_gram):
    vmem = pl.BlockSpec(memory_space=pltpu.VMEM)
    hbm = pl.BlockSpec(memory_space=pltpu.HBM)
    bf16, f32 = jnp.bfloat16, jnp.float32
    slots = SHARDS * CAP
    rows = (KEPT, 8, W)
    outs = [jax.ShapeDtypeStruct(x.shape, x.dtype) for x in (grad, avg, avg_sq, left_gram, right_gram)]
    operands = [
        pltpu.with_memory_space_constraint(x, pltpu.HBM)
        for x in (owner.T, left_basis, right_basis, avg, avg_sq, grad, left_gram, right_gram)
    ]
    results = pl.pallas_call(
        kernel,
        out_shape=[jax.ShapeDtypeStruct((KEPT, W, W), bf16)] + outs[1:],
        in_specs=[hbm] * 8,
        out_specs=[vmem] * 5,
        scratch_shapes=[
            pltpu.VMEM(owner.shape[::-1], jnp.int32),
            pltpu.VMEM((8, 128), jnp.int32),
            pltpu.SMEM((8, 128), jnp.int32),
            pltpu.VMEM(rows, bf16),
            pltpu.VMEM(rows, bf16),
            pltpu.VMEM(rows, bf16),
            pltpu.VMEM(rows, f32),
            pltpu.VMEM(grad.shape, bf16),
            pltpu.VMEM(rows, f32),
            pltpu.VMEM(rows, f32),
            pltpu.VMEM((KEPT, 2, PR, PC), bf16),
            pltpu.VMEM((slots, 2, PR, PC), bf16),
            pltpu.VMEM((slots, 2, PR, PC), bf16),
            pltpu.VMEM((slots, 2, PR, PC), bf16),
            pltpu.VMEM((slots, 2, PR, PC), bf16),
            pltpu.VMEM((KEPT, 2, PR, PC), bf16),
            pltpu.VMEM((KEPT, 2, PR, PC), bf16),
            pltpu.VMEM((REPS, 2, PR, PC), bf16),
            pltpu.VMEM((REPS, 2, PR, PC), bf16),
            pltpu.VMEM((REPS, PR, PC), bf16),
            pltpu.VMEM((KEPT, PR, PC), bf16),
            pltpu.VMEM((KEPT, 2, PR, PC), bf16),
            pltpu.VMEM((slots, 3, PR, PC), bf16),
            pltpu.VMEM((slots, 3, PR, PC), bf16),
            pltpu.SemaphoreType.DMA((8,)),
            pltpu.SemaphoreType.DMA,
            pltpu.SemaphoreType.DMA((6,)),
            pltpu.SemaphoreType.DMA((6,)),
            pltpu.SemaphoreType.DMA((3 * PARTS,)),
            pltpu.SemaphoreType.DMA((18 * PARTS,)),
            pltpu.SemaphoreType.DMA((18 * PARTS,)),
        ],
        compiler_params=pltpu.CompilerParams(
            collective_id=0, has_side_effects=True, vmem_limit_bytes=40 * 1024 * 1024
        ),
        cost_estimate=pl.CostEstimate(flops=12 * W**3, bytes_accessed=6 << 20, transcendentals=0),
        name="soap_step",
    )(*operands)
    return tuple(
        pl.pallas_call(
            store_kernel,
            out_shape=outs,
            in_specs=[pl.BlockSpec(memory_space=pl.ANY)] * 5,
            out_specs=[hbm] * 5,
            scratch_shapes=[pltpu.SemaphoreType.DMA((KEPT + 4,))],
            compiler_params=pltpu.CompilerParams(vmem_limit_bytes=4 * 1024 * 1024),
            cost_estimate=pl.CostEstimate(flops=0, bytes_accessed=5 << 20, transcendentals=0),
            name="store",
        )(*results)
    )


def solution(mesh):
    rows = P("shard", "rep", None)
    return jax.shard_map(
        body,
        mesh=mesh,
        in_specs=(P("shard", None), P(), rows, rows, rows, rows, rows, rows),
        out_specs=(P("shard", None), rows, rows, rows, rows),
        check_vma=False,
    )
```

```python
import functools

import jax
import jax.numpy as jnp
from jax import lax
from jax.experimental import pallas as pl
from jax.experimental.pallas import tpu as pltpu
from jax.sharding import PartitionSpec as P

CAP = 2
BETA_ONE = 0.9
BETA_TWO = 0.95
EPSILON = 1e-08

YS = 8
ZS = 4
REPS = YS * ZS
SHARDS = 16
KEPT = 16
W = 256
PR, PC = 16, 128
PARTS = 2
FAR_Y = (4, 3, 5, 2, 6, 1, 7, 0)
FAR_Z = (2, 1, 3, 0)
MESH = pl.DeviceIdType.MESH


def routing(owner_t, here):
    i32, f32 = jnp.int32, jnp.float32
    count = owner_t.shape[0] * owner_t.shape[1]
    cols, rows = owner_t.shape
    square = lax.broadcasted_iota(i32, (rows, rows), 0) == lax.broadcasted_iota(i32, (rows, rows), 1)

    def total(mask, value, axis):
        return jnp.sum(jnp.where(mask, value, 0).astype(f32), axis=axis, keepdims=True).astype(i32)

    def numbers(shape, axis):
        at = lax.broadcasted_iota(i32, shape, axis)
        return at % rows * cols + at // rows, at % rows * cols // KEPT

    flat = jnp.concatenate([total(square, owner_t[j : j + 1, :], 1) for j in range(cols)], axis=0)
    ident, source = numbers((count, 1), 0)
    ident_r, source_r = numbers((1, count), 1)
    diagonal = ident == ident_r
    flat_r = total(diagonal, flat, 0)
    same = (flat == flat_r) & (ident_r < ident)
    rank = total(same, 1, 1)
    pair = total(same & (source == source_r), 1, 1)
    to_slot, from_slot = flat * CAP + pair, source * CAP + pair
    lane = lax.broadcasted_iota(i32, (1, 128), 1)
    slots = SHARDS * CAP
    owned = flat == here
    picked = jnp.where(
        lane < slots,
        jnp.where((source == here) & (to_slot == lane), ident - here * KEPT, 0),
        jnp.where(
            lane < slots + KEPT,
            jnp.where(owned & (rank == lane - slots), from_slot, 0),
            jnp.where(
                lane < 2 * slots + KEPT,
                jnp.where(owned & (from_slot == lane - slots - KEPT), rank, 0),
                jnp.where(ident == here * KEPT + lane - 2 * slots - KEPT, to_slot, 0),
            ),
        ),
    )
    row = jnp.sum(picked.astype(f32), axis=0, keepdims=True).astype(i32)
    of_slots = ((lane >= slots) & (lane < slots + KEPT)) | (lane >= 2 * slots + KEPT)
    row = jnp.maximum(jnp.minimum(row, jnp.where(of_slots, slots - 1, KEPT - 1)), 0)
    return jnp.broadcast_to(row, (8, 128))


def fold(x):
    x = x.astype(jnp.float32)
    return jnp.concatenate([x[:, :, :PC], x[:, :, PC:]], axis=1).astype(jnp.bfloat16)


def unfold(x):
    x = x.astype(jnp.float32)
    return jnp.concatenate([x[:, :8, :], x[:, 8:, :]], axis=2)


def nn(a, b):
    return lax.dot_general(a, b, (((1,), (0,)), ((), ())), preferred_element_type=jnp.float32)


def nt(a, b):
    return lax.dot_general(a, b, (((1,), (1,)), ((), ())), preferred_element_type=jnp.float32)


def tn(a, b):
    return lax.dot_general(a, b, (((0,), (0,)), ((), ())), preferred_element_type=jnp.float32)


def wait_bytes(ref, sem):
    pltpu.make_async_copy(ref, ref, sem).wait()


def kernel(
    owner_h, left_h, right_h, avg_h, avg_sq_h, grad, left_gram_h, right_gram_h,
    update, new_avg, new_avg_sq, new_left, new_right,
    owner, table_v, table, left, right, avg, avg_sq, whole, left_gram, right_gram,
    folded, bases_out, moments_out, bases_in, moments_in, bases_row, moments_row, bases, moments,
    rsend, rbuf, grams, tsend, trecv,
    load_sem, table_sem, send_sem, recv_sem, z_send, ag_send, ag_recv,
):
    r = lax.axis_index("rep")
    s = lax.axis_index("shard")
    y, z = r // ZS, r % ZS
    z_half, z_odd = z // 2, z % 2
    p0 = (y + s) % 2
    is_hub = z_odd == p0

    def wrap(v, n):
        return jnp.where(v >= n, v - n, v)

    ys = [wrap(y + t, YS) for t in range(YS)]
    zs = [wrap(z + t, ZS) for t in range(ZS)]
    z_low, x, core = s // 8, s % 8 // 2, s % 2
    xs = [wrap(x + t, 4) for t in range(4)]
    moves = (
        (1, 2, 1), (1, 2, 0), (0, 2, 1), (0, 2, 0), (1, 1, 1), (1, 1, 0), (1, 3, 1), (1, 3, 0),
        (0, 1, 1), (0, 1, 0), (0, 3, 1), (0, 3, 0), (1, 0, 1), (1, 0, 0), (0, 0, 1),
    )
    ss = [
        (1 - z_low if a else z_low) * 8 + xs[b] * 2 + (1 - core if c else core) for a, b, c in moves
    ]
    r_out = y * ZS + jnp.where(z_low == 1, zs[1], zs[3])

    def to(rep):
        return dict(device_id={"rep": rep}, device_id_type=MESH)

    def over(shard):
        return dict(device_id={"shard": shard}, device_id_type=MESH)

    loads = [
        pltpu.make_async_copy(src, dst, load_sem.at[n])
        for n, (src, dst) in enumerate(
            [(left_h, left), (right_h, right), (avg_h, avg), (avg_sq_h, avg_sq),
             (grad, whole), (left_gram_h, left_gram), (right_gram_h, right_gram), (owner_h, owner)]
        )
    ]
    for copy in (loads[7], *loads[:4]):
        copy.start()

    def idx(n):
        return table[0, n]

    barrier = pltpu.get_barrier_semaphore()
    def outside(peer):
        return dict(device_id={"rep": r_out, "shard": peer}, device_id_type=MESH)

    for peer, move in zip(ss, moves):
        pl.semaphore_signal(barrier, inc=1, **over(peer))
        if move[0]:
            pl.semaphore_signal(barrier, inc=1, **outside(peer))

    @pl.when(is_hub)
    def _():
        for t in FAR_Y:
            for v in FAR_Z:
                if t or v:
                    pl.semaphore_signal(barrier, inc=1, **to(ys[t] * ZS + zs[v]))

    loads[7].wait()
    table_v[...] = routing(owner[...], s)
    pltpu.make_async_copy(table_v, table, table_sem).start()

    def pack(first, refs, out):
        for n, ref in enumerate(refs):
            loads[first + n].wait()
            folded[:, n] = fold(ref[...])
        if first == 0:
            pltpu.make_async_copy(table_v, table, table_sem).wait()
        for n in range(SHARDS * CAP):
            out[n] = folded[idx(SHARDS * CAP + KEPT + n)]

    pack(0, (left, right), bases_out)
    pl.semaphore_wait(barrier, jnp.where(is_hub, SHARDS - 1 + 8 + KEPT - 1, SHARDS - 1 + 8 + KEPT))

    mine = pl.ds(s * CAP, CAP)

    def exchange(src, dst, n, turned=False):
        pltpu.make_async_copy(src.at[mine], dst.at[mine], recv_sem.at[n]).start()
        for peer, move in zip(ss, moves):
            pltpu.make_async_remote_copy(
                src.at[pl.ds(peer * CAP, CAP)], dst.at[mine], send_sem.at[n], recv_sem.at[n],
                **(outside(peer) if turned and move[0] else over(peer)),
            ).start()

    exchange(bases_out, bases_in, 0)
    pack(2, (avg, avg_sq), moments_out)
    exchange(moments_out, moments_in, 1, turned=True)
    for copy in loads[4:7]:
        copy.start()

    strip_at = pl.multiple_of(PR * (2 * y + z_half), PR)
    picks = (
        lax.broadcasted_iota(jnp.int32, (PR, W), 1)
        == lax.broadcasted_iota(jnp.int32, (PR, W), 0) + strip_at
    ).astype(jnp.float32).astype(jnp.bfloat16)

    def gram_rows(blocks):
        for b in blocks:
            i, j = b // 8, b % 8
            g = whole[i * W : (i + 1) * W, j * W : (j + 1) * W]
            strip = whole[pl.ds(i * W + strip_at, PR), j * W : (j + 1) * W]
            both = nt(jnp.concatenate([strip, picks], axis=0), g)
            wide = nn(both[PR:].astype(jnp.bfloat16), g)
            for n, v in enumerate((both[:PR], wide)):
                v = jnp.where(z_odd == 1, v[8:], v[:8])
                grams[b, n] = jnp.concatenate([v[:, :PC], v[:, PC:]], axis=0).astype(jnp.bfloat16)

    def to_hub(src, dst, n):
        for t in FAR_Y:
            p = p0 if t % 2 == 0 else 1 - p0
            for b in (1 - z_half, z_half):
                block, h = 2 * ys[t] + b, ys[t] * ZS + 2 * b + p

                def remote(block=block, h=h):
                    pltpu.make_async_remote_copy(
                        src.at[block], dst.at[r], send_sem.at[n], recv_sem.at[n], **to(h)
                    ).start()

                if t == 0:
                    pl.when(h != r)(remote)

                    @pl.when(h == r)
                    def _(block=block):
                        pltpu.make_async_copy(src.at[block], dst.at[r], recv_sem.at[n]).start()
                else:
                    remote()

    loads[4].wait()
    gram_rows(range(0, 6))
    for n, (got, row, out) in enumerate(
        ((bases_in, bases_row, bases), (moments_in, moments_row, moments))
    ):
        wait_bytes(got, recv_sem.at[n])
        for b in range(KEPT):
            row[b] = got[idx(2 * SHARDS * CAP + KEPT + b)]
        to_hub(row, out, 2 + n)
        gram_rows(range(6, 10) if n == 0 else range(10, KEPT))

    block_me = 2 * y + z_half

    @pl.when(is_hub)
    def _():
        g = whole[
            pl.ds(pl.multiple_of(y // 4 * W, W), W),
            pl.ds(pl.multiple_of(y % 4 * (2 * W) + z_half * W, W), W),
        ]
        wait_bytes(bases, recv_sem.at[2])
        lb = unfold(bases[:, 0]).reshape(W, W).astype(jnp.bfloat16)
        rb = unfold(bases[:, 1]).reshape(W, W).astype(jnp.bfloat16)
        half = nn(lb, g).astype(jnp.bfloat16)
        turned = nn(half, rb)
        wait_bytes(moments, recv_sem.at[3])
        crossed = idx(2 * SHARDS * CAP + KEPT + block_me) // (8 * CAP) != z_low

        def in_order(x):
            x = unfold(x).reshape(YS, ZS, 8, W)
            up = jnp.concatenate([x[:, ZS - 1 :], x[:, : ZS - 1]], axis=1)
            down = jnp.concatenate([x[:, 1:], x[:, :1]], axis=1)
            x = jnp.where(crossed, jnp.where(z_low == 1, up, down), x)
            return x.reshape(W, W)

        m0 = in_order(moments[:, 0])
        v0 = in_order(moments[:, 1])
        first = BETA_ONE * m0 + (1.0 - BETA_ONE) * turned
        second = BETA_TWO * v0 + (1.0 - BETA_TWO) * turned * turned
        scaled = (first / (jnp.sqrt(second) + EPSILON)).astype(jnp.bfloat16)
        back = nt(scaled, rb).astype(jnp.bfloat16)
        update[block_me] = tn(lb, back).astype(jnp.bfloat16)
        rsend[...] = fold(turned.reshape(REPS, 8, W))

    ups = (ys[1] * ZS + z, ys[7] * ZS + z)
    z_pair = 2 * z_half + 1 - z_odd
    z_next = jnp.where(z_odd == 1, zs[1], zs[3])
    pending = []
    names = {}

    def region(t, bit, rows):
        return update.at[2 * ys[t] + bit, pl.ds(rows[0], rows[1] - rows[0])]

    def push(ref, peer, key):
        n = names.setdefault(key, len(names))
        copy = pltpu.make_async_remote_copy(ref, ref, ag_send.at[n], ag_recv.at[n], **to(peer))
        copy.start()
        return copy

    def pull(ref, key):
        wait_bytes(ref, ag_recv.at[names[key]])

    bits = (z_half, 1 - z_half)
    parts = [(n * W // PARTS, (n + 1) * W // PARTS) for n in range(PARTS)]

    @pl.when(is_hub)
    def _():
        for m, rows in enumerate(parts):
            ref = region(0, bits[0], rows)
            for n, (c, peer) in enumerate(((1, zs[2]), (1, z_next), (0, z_pair))):
                key = names.setdefault(("z", c, m), len(names))
                pltpu.make_async_remote_copy(
                    ref, ref, z_send.at[3 * m + n], ag_recv.at[key], **to(y * ZS + peer)
                ).start()

    def y_rows(m, d, way):
        lo, hi = parts[m]
        if d < YS // 2:
            return lo, hi
        mid = (lo + hi) // 2
        return (lo, mid) if way == 0 else (mid, hi)

    def far(d, way):
        return (-d if way == 0 else d) % YS

    def y_push(c, m, d, way):
        ref = region(far(d - 1, way), bits[c], y_rows(m, d, way))
        pending.append(push(ref, ups[way], ("y", c, m, d, way)))

    def z_step(c, m):
        ref = region(0, bits[c], parts[m])
        if c == 0:
            pl.when(jnp.logical_not(is_hub))(lambda: pull(ref, ("z", c, m)))
        else:
            pull(ref, ("z", c, m))
        for way in range(2):
            y_push(c, m, 1, way)

    def y_step(c, m, d):
        for way in range(2):
            pull(region(far(d, way), bits[c], y_rows(m, d, way)), ("y", c, m, d, way))
            if d < YS // 2:
                y_push(c, m, d + 1, way)

    def send_r():
        @pl.when(is_hub)
        def _():
            for t in FAR_Y:
                for v in FAR_Z:
                    q = ys[t] * ZS + zs[v]
                    if t or v:
                        pltpu.make_async_remote_copy(
                            rsend.at[q], rbuf.at[block_me], send_sem.at[4], recv_sem.at[4], **to(q)
                        ).start()
                    else:
                        pltpu.make_async_copy(rsend.at[r], rbuf.at[block_me], recv_sem.at[4]).start()

    def to_owners():
        wait_bytes(rbuf, recv_sem.at[4])
        for m in range(SHARDS * CAP):
            b = idx(m)
            tsend[m, 0] = rbuf[b]
            tsend[m, 1:] = grams[b]
        exchange(tsend, trecv, 5)

    def own_rows():
        wait_bytes(trecv, recv_sem.at[5])
        for copy in loads[5:7]:
            copy.wait()
        for n in range(KEPT):
            turned, gl, gr = unfold(trecv[idx(SHARDS * CAP + n)])
            new_avg[n] = (BETA_ONE * avg[n].astype(jnp.float32) + (1.0 - BETA_ONE) * turned).astype(jnp.bfloat16)
            new_avg_sq[n] = BETA_TWO * avg_sq[n] + (1.0 - BETA_TWO) * turned * turned
            new_left[n] = BETA_TWO * left_gram[n] + (1.0 - BETA_TWO) * gl
            new_right[n] = BETA_TWO * right_gram[n] + (1.0 - BETA_TWO) * gr

    order = [(z_step, 0, m) for m in range(PARTS)]
    for m in range(PARTS):
        order += [(z_step, 1, m), (y_step, 0, m, 1)]
    order += [(y_step, 1, m, 1) for m in range(PARTS)]
    for d in (2, 3, 4):
        order += [(y_step, c, m, d) for c in range(2) for m in range(PARTS)]
    for count, (step, *args) in enumerate(order[:-2]):
        step(*args)
        if count == PARTS - 1:
            send_r()
        if count == 4 * PARTS:
            to_owners()
        if count == len(order) - 4:
            own_rows()

    for copy in pending:
        copy.wait_send()
    for n, ref in ((0, bases_out), (1, moments_out), (5, tsend)):
        wait_bytes(ref.at[pl.ds(0, CAP * (SHARDS - 1))], send_sem.at[n])

    @pl.when(is_hub)
    def _():
        wait_bytes(bases_row.at[pl.ds(0, KEPT - 1)], send_sem.at[2])
        wait_bytes(moments_row.at[pl.ds(0, KEPT - 1)], send_sem.at[3])
        wait_bytes(rsend.at[pl.ds(0, REPS - 1)], send_sem.at[4])
        for n in range(3 * PARTS):
            wait_bytes(region(0, bits[0], parts[n // 3]), z_send.at[n])

    @pl.when(jnp.logical_not(is_hub))
    def _():
        wait_bytes(bases_row, send_sem.at[2])
        wait_bytes(moments_row, send_sem.at[3])

    for step, *args in order[-2:]:
        step(*args)


def store_kernel(*refs):
    count = len(refs) // 2
    sems = refs[-1]
    copies = []
    for n in range(count):
        src, dst = refs[n], refs[count + n]
        if n == 0:
            for b in range(KEPT):
                i, j = b // 8, b % 8
                place = dst.at[i * W : (i + 1) * W, j * W : (j + 1) * W]
                copies.append(pltpu.make_async_copy(src.at[b], place, sems.at[len(copies)]))
        else:
            copies.append(pltpu.make_async_copy(src, dst, sems.at[len(copies)]))
    for copy in copies:
        copy.start()
    for copy in copies:
        copy.wait()


def body(grad, owner, left_basis, right_basis, avg, avg_sq, left_gram, right_gram):
    vmem = pl.BlockSpec(memory_space=pltpu.VMEM)
    hbm = pl.BlockSpec(memory_space=pltpu.HBM)
    bf16, f32 = jnp.bfloat16, jnp.float32
    slots = SHARDS * CAP
    rows = (KEPT, 8, W)
    outs = [jax.ShapeDtypeStruct(x.shape, x.dtype) for x in (grad, avg, avg_sq, left_gram, right_gram)]
    operands = [
        pltpu.with_memory_space_constraint(x, pltpu.HBM)
        for x in (owner.T, left_basis, right_basis, avg, avg_sq, grad, left_gram, right_gram)
    ]
    results = pl.pallas_call(
        kernel,
        out_shape=[jax.ShapeDtypeStruct((KEPT, W, W), bf16)] + outs[1:],
        in_specs=[hbm] * 8,
        out_specs=[vmem] * 5,
        scratch_shapes=[
            pltpu.VMEM(owner.shape[::-1], jnp.int32),
            pltpu.VMEM((8, 128), jnp.int32),
            pltpu.SMEM((8, 128), jnp.int32),
            pltpu.VMEM(rows, bf16),
            pltpu.VMEM(rows, bf16),
            pltpu.VMEM(rows, bf16),
            pltpu.VMEM(rows, f32),
            pltpu.VMEM(grad.shape, bf16),
            pltpu.VMEM(rows, f32),
            pltpu.VMEM(rows, f32),
            pltpu.VMEM((KEPT, 2, PR, PC), bf16),
            pltpu.VMEM((slots, 2, PR, PC), bf16),
            pltpu.VMEM((slots, 2, PR, PC), bf16),
            pltpu.VMEM((slots, 2, PR, PC), bf16),
            pltpu.VMEM((slots, 2, PR, PC), bf16),
            pltpu.VMEM((KEPT, 2, PR, PC), bf16),
            pltpu.VMEM((KEPT, 2, PR, PC), bf16),
            pltpu.VMEM((REPS, 2, PR, PC), bf16),
            pltpu.VMEM((REPS, 2, PR, PC), bf16),
            pltpu.VMEM((REPS, PR, PC), bf16),
            pltpu.VMEM((KEPT, PR, PC), bf16),
            pltpu.VMEM((KEPT, 2, PR, PC), bf16),
            pltpu.VMEM((slots, 3, PR, PC), bf16),
            pltpu.VMEM((slots, 3, PR, PC), bf16),
            pltpu.SemaphoreType.DMA((8,)),
            pltpu.SemaphoreType.DMA,
            pltpu.SemaphoreType.DMA((6,)),
            pltpu.SemaphoreType.DMA((6,)),
            pltpu.SemaphoreType.DMA((3 * PARTS,)),
            pltpu.SemaphoreType.DMA((18 * PARTS,)),
            pltpu.SemaphoreType.DMA((18 * PARTS,)),
        ],
        compiler_params=pltpu.CompilerParams(
            collective_id=0, has_side_effects=True, vmem_limit_bytes=40 * 1024 * 1024
        ),
        cost_estimate=pl.CostEstimate(flops=12 * W**3, bytes_accessed=6 << 20, transcendentals=0),
        name="soap_step",
    )(*operands)
    return tuple(
        pl.pallas_call(
            store_kernel,
            out_shape=outs,
            in_specs=[pl.BlockSpec(memory_space=pl.ANY)] * 5,
            out_specs=[hbm] * 5,
            scratch_shapes=[pltpu.SemaphoreType.DMA((KEPT + 4,))],
            compiler_params=pltpu.CompilerParams(vmem_limit_bytes=4 * 1024 * 1024),
            cost_estimate=pl.CostEstimate(flops=0, bytes_accessed=5 << 20, transcendentals=0),
            name="store",
        )(*results)
    )


def solution(mesh):
    rows = P("shard", "rep", None)
    return jax.shard_map(
        body,
        mesh=mesh,
        in_specs=(P("shard", None), P(), rows, rows, rows, rows, rows, rows),
        out_specs=(P("shard", None), rows, rows, rows, rows),
        check_vma=False,
    )
```

```python
import functools

import jax
import jax.numpy as jnp
from jax import lax
from jax.experimental import pallas as pl
from jax.experimental.pallas import tpu as pltpu
from jax.sharding import PartitionSpec as P

CAP = 2
BETA_ONE = 0.9
BETA_TWO = 0.95
EPSILON = 1e-08

YS = 8
ZS = 4
REPS = YS * ZS
SHARDS = 16
KEPT = 16
W = 256
PR, PC = 16, 128
PARTS = 2
FAR_Y = (4, 3, 5, 2, 6, 1, 7, 0)
FAR_Z = (2, 1, 3, 0)
MESH = pl.DeviceIdType.MESH


def routing(owner_t, here):
    i32, f32 = jnp.int32, jnp.float32
    count = owner_t.shape[0] * owner_t.shape[1]
    cols, rows = owner_t.shape
    square = lax.broadcasted_iota(i32, (rows, rows), 0) == lax.broadcasted_iota(i32, (rows, rows), 1)

    def total(mask, value, axis):
        return jnp.sum(jnp.where(mask, value, 0).astype(f32), axis=axis, keepdims=True).astype(i32)

    def numbers(shape, axis):
        at = lax.broadcasted_iota(i32, shape, axis)
        return at % rows * cols + at // rows, at % rows * cols // KEPT

    flat = jnp.concatenate([total(square, owner_t[j : j + 1, :], 1) for j in range(cols)], axis=0)
    ident, source = numbers((count, 1), 0)
    ident_r, source_r = numbers((1, count), 1)
    diagonal = ident == ident_r
    flat_r = total(diagonal, flat, 0)
    same = (flat == flat_r) & (ident_r < ident)
    rank = total(same, 1, 1)
    pair = total(same & (source == source_r), 1, 1)
    to_slot, from_slot = flat * CAP + pair, source * CAP + pair
    lane = lax.broadcasted_iota(i32, (1, 128), 1)
    slots = SHARDS * CAP
    owned = flat == here
    picked = jnp.where(
        lane < slots,
        jnp.where((source == here) & (to_slot == lane), ident - here * KEPT, 0),
        jnp.where(
            lane < slots + KEPT,
            jnp.where(owned & (rank == lane - slots), from_slot, 0),
            jnp.where(
                lane < 2 * slots + KEPT,
                jnp.where(owned & (from_slot == lane - slots - KEPT), rank, 0),
                jnp.where(ident == here * KEPT + lane - 2 * slots - KEPT, to_slot, 0),
            ),
        ),
    )
    row = jnp.sum(picked.astype(f32), axis=0, keepdims=True).astype(i32)
    of_slots = ((lane >= slots) & (lane < slots + KEPT)) | (lane >= 2 * slots + KEPT)
    row = jnp.maximum(jnp.minimum(row, jnp.where(of_slots, slots - 1, KEPT - 1)), 0)
    return jnp.broadcast_to(row, (8, 128))


def fold(x):
    x = x.astype(jnp.float32)
    return jnp.concatenate([x[:, :, :PC], x[:, :, PC:]], axis=1).astype(jnp.bfloat16)


def unfold(x):
    x = x.astype(jnp.float32)
    return jnp.concatenate([x[:, :8, :], x[:, 8:, :]], axis=2)


def nn(a, b):
    return lax.dot_general(a, b, (((1,), (0,)), ((), ())), preferred_element_type=jnp.float32)


def nt(a, b):
    return lax.dot_general(a, b, (((1,), (1,)), ((), ())), preferred_element_type=jnp.float32)


def tn(a, b):
    return lax.dot_general(a, b, (((0,), (0,)), ((), ())), preferred_element_type=jnp.float32)


def wait_bytes(ref, sem):
    pltpu.make_async_copy(ref, ref, sem).wait()


def kernel(
    owner_h, left_h, right_h, avg_h, avg_sq_h, grad, left_gram_h, right_gram_h,
    update, new_avg, new_avg_sq, new_left, new_right,
    owner, table_v, table, left, right, avg, avg_sq, whole, left_gram, right_gram,
    folded, bases_out, moments_out, bases_in, moments_in, bases_row, moments_row, bases, moments,
    rsend, rbuf, grams, tsend, trecv, r_send, r_recv,
    load_sem, table_sem, send_sem, recv_sem, z_send, ag_send, ag_recv,
):
    r = lax.axis_index("rep")
    s = lax.axis_index("shard")
    y, z = r // ZS, r % ZS
    z_half, z_odd = z // 2, z % 2
    p0 = (y + s) % 2
    is_hub = z_odd == p0

    def wrap(v, n):
        return jnp.where(v >= n, v - n, v)

    ys = [wrap(y + t, YS) for t in range(YS)]
    zs = [wrap(z + t, ZS) for t in range(ZS)]
    z_low, x, core = s // 8, s % 8 // 2, s % 2
    xs = [wrap(x + t, 4) for t in range(4)]
    ss = [
        (1 - z_low if a else z_low) * 8 + xs[b] * 2 + (1 - core if c else core)
        for a, b, c in (
            (1, 2, 1), (1, 2, 0), (0, 2, 1), (0, 2, 0), (1, 1, 1), (1, 1, 0), (1, 3, 1), (1, 3, 0),
            (0, 1, 1), (0, 1, 0), (0, 3, 1), (0, 3, 0), (1, 0, 1), (1, 0, 0), (0, 0, 1),
        )
    ]

    def to(rep):
        return dict(device_id={"rep": rep}, device_id_type=MESH)

    def over(shard):
        return dict(device_id={"shard": shard}, device_id_type=MESH)

    loads = [
        pltpu.make_async_copy(src, dst, load_sem.at[n])
        for n, (src, dst) in enumerate(
            [(left_h, left), (right_h, right), (avg_h, avg), (avg_sq_h, avg_sq),
             (grad, whole), (left_gram_h, left_gram), (right_gram_h, right_gram), (owner_h, owner)]
        )
    ]
    for copy in (loads[7], *loads[:4]):
        copy.start()

    def idx(n):
        return table[0, n]

    barrier = pltpu.get_barrier_semaphore()
    for peer in ss:
        pl.semaphore_signal(barrier, inc=1, **over(peer))

    @pl.when(is_hub)
    def _():
        for t in FAR_Y:
            for v in FAR_Z:
                if t or v:
                    pl.semaphore_signal(barrier, inc=1, **to(ys[t] * ZS + zs[v]))

    loads[7].wait()
    table_v[...] = routing(owner[...], s)
    pltpu.make_async_copy(table_v, table, table_sem).start()

    def pack(first, refs, out):
        for n, ref in enumerate(refs):
            loads[first + n].wait()
            folded[:, n] = fold(ref[...])
        if first == 0:
            pltpu.make_async_copy(table_v, table, table_sem).wait()
        for n in range(SHARDS * CAP):
            out[n] = folded[idx(SHARDS * CAP + KEPT + n)]

    pack(0, (left, right), bases_out)
    pl.semaphore_wait(barrier, jnp.where(is_hub, SHARDS - 1 + KEPT - 1, SHARDS - 1 + KEPT))

    mine = pl.ds(s * CAP, CAP)

    def exchange(src, dst, n):
        pltpu.make_async_copy(src.at[mine], dst.at[mine], recv_sem.at[n]).start()
        for peer in ss:
            pltpu.make_async_remote_copy(
                src.at[pl.ds(peer * CAP, CAP)], dst.at[mine], send_sem.at[n], recv_sem.at[n], **over(peer)
            ).start()

    exchange(bases_out, bases_in, 0)
    pack(2, (avg, avg_sq), moments_out)
    exchange(moments_out, moments_in, 1)
    for copy in loads[4:7]:
        copy.start()

    strip_at = pl.multiple_of(PR * (2 * y + z_half), PR)
    picks = (
        lax.broadcasted_iota(jnp.int32, (PR, W), 1)
        == lax.broadcasted_iota(jnp.int32, (PR, W), 0) + strip_at
    ).astype(jnp.float32).astype(jnp.bfloat16)

    def gram_rows(blocks):
        for b in blocks:
            i, j = b // 8, b % 8
            g = whole[i * W : (i + 1) * W, j * W : (j + 1) * W]
            strip = whole[pl.ds(i * W + strip_at, PR), j * W : (j + 1) * W]
            both = nt(jnp.concatenate([strip, picks], axis=0), g)
            wide = nn(both[PR:].astype(jnp.bfloat16), g)
            for n, v in enumerate((both[:PR], wide)):
                v = jnp.where(z_odd == 1, v[8:], v[:8])
                grams[b, n] = jnp.concatenate([v[:, :PC], v[:, PC:]], axis=0).astype(jnp.bfloat16)

    def to_hub(src, dst, n):
        for t in FAR_Y:
            p = p0 if t % 2 == 0 else 1 - p0
            for b in (1 - z_half, z_half):
                block, h = 2 * ys[t] + b, ys[t] * ZS + 2 * b + p

                def remote(block=block, h=h):
                    pltpu.make_async_remote_copy(
                        src.at[block], dst.at[r], send_sem.at[n], recv_sem.at[n], **to(h)
                    ).start()

                if t == 0:
                    pl.when(h != r)(remote)

                    @pl.when(h == r)
                    def _(block=block):
                        pltpu.make_async_copy(src.at[block], dst.at[r], recv_sem.at[n]).start()
                else:
                    remote()

    loads[4].wait()
    gram_rows(range(0, 4))
    for n, (got, row, out) in enumerate(
        ((bases_in, bases_row, bases), (moments_in, moments_row, moments))
    ):
        wait_bytes(got, recv_sem.at[n])
        for b in range(KEPT):
            row[b] = got[idx(2 * SHARDS * CAP + KEPT + b)]
        to_hub(row, out, 2 + n)
        if n == 0:
            gram_rows(range(4, 9))

    def grams_to_owners():
        gram_rows(range(9, KEPT))
        for m in range(SHARDS * CAP):
            tsend[m] = grams[idx(m)]
        exchange(tsend, trecv, 5)

    pl.when(jnp.logical_not(is_hub))(grams_to_owners)

    block_me = 2 * y + z_half

    @pl.when(is_hub)
    def _():
        g = whole[
            pl.ds(pl.multiple_of(y // 4 * W, W), W),
            pl.ds(pl.multiple_of(y % 4 * (2 * W) + z_half * W, W), W),
        ]
        wait_bytes(bases, recv_sem.at[2])
        lb = unfold(bases[:, 0]).reshape(W, W).astype(jnp.bfloat16)
        rb = unfold(bases[:, 1]).reshape(W, W).astype(jnp.bfloat16)
        half = nn(lb, g).astype(jnp.bfloat16)
        turned = nn(half, rb)
        wait_bytes(moments, recv_sem.at[3])
        m0 = unfold(moments[:, 0]).reshape(W, W)
        v0 = unfold(moments[:, 1]).reshape(W, W)
        first = BETA_ONE * m0 + (1.0 - BETA_ONE) * turned
        second = BETA_TWO * v0 + (1.0 - BETA_TWO) * turned * turned
        scaled = (first / (jnp.sqrt(second) + EPSILON)).astype(jnp.bfloat16)
        back = nt(scaled, rb).astype(jnp.bfloat16)
        update[block_me] = tn(lb, back).astype(jnp.bfloat16)
        rsend[...] = fold(turned.reshape(REPS, 8, W))

    ups = (ys[1] * ZS + z, ys[7] * ZS + z)
    z_pair = 2 * z_half + 1 - z_odd
    z_next = jnp.where(z_odd == 1, zs[1], zs[3])
    pending = []
    names = {}

    def region(t, bit, rows):
        return update.at[2 * ys[t] + bit, pl.ds(rows[0], rows[1] - rows[0])]

    def push(ref, peer, key):
        n = names.setdefault(key, len(names))
        copy = pltpu.make_async_remote_copy(ref, ref, ag_send.at[n], ag_recv.at[n], **to(peer))
        copy.start()
        return copy

    def pull(ref, key):
        wait_bytes(ref, ag_recv.at[names[key]])

    bits = (z_half, 1 - z_half)
    parts = [(n * W // PARTS, (n + 1) * W // PARTS) for n in range(PARTS)]

    @pl.when(is_hub)
    def _():
        for m, rows in enumerate(parts):
            ref = region(0, bits[0], rows)
            for n, (c, peer) in enumerate(((1, zs[2]), (1, z_next), (0, z_pair))):
                key = names.setdefault(("z", c, m), len(names))
                pltpu.make_async_remote_copy(
                    ref, ref, z_send.at[3 * m + n], ag_recv.at[key], **to(y * ZS + peer)
                ).start()

    def y_rows(m, d, way):
        lo, hi = parts[m]
        if d < YS // 2:
            return lo, hi
        mid = (lo + hi) // 2
        return (lo, mid) if way == 0 else (mid, hi)

    def far(d, way):
        return (-d if way == 0 else d) % YS

    def y_push(c, m, d, way):
        ref = region(far(d - 1, way), bits[c], y_rows(m, d, way))
        pending.append(push(ref, ups[way], ("y", c, m, d, way)))

    def z_step(c, m):
        ref = region(0, bits[c], parts[m])
        if c == 0:
            pl.when(jnp.logical_not(is_hub))(lambda: pull(ref, ("z", c, m)))
        else:
            pull(ref, ("z", c, m))
        for way in range(2):
            y_push(c, m, 1, way)

    def y_step(c, m, d):
        for way in range(2):
            pull(region(far(d, way), bits[c], y_rows(m, d, way)), ("y", c, m, d, way))
            if d < YS // 2:
                y_push(c, m, d + 1, way)

    def send_r():
        @pl.when(is_hub)
        def _():
            for t in FAR_Y:
                for v in FAR_Z:
                    q = ys[t] * ZS + zs[v]
                    if t or v:
                        pltpu.make_async_remote_copy(
                            rsend.at[q], rbuf.at[block_me], send_sem.at[4], recv_sem.at[4], **to(q)
                        ).start()
                    else:
                        pltpu.make_async_copy(rsend.at[r], rbuf.at[block_me], recv_sem.at[4]).start()

    def to_owners():
        wait_bytes(rbuf, recv_sem.at[4])
        for m in range(SHARDS * CAP):
            r_send[m] = rbuf[idx(m)]
        exchange(r_send, r_recv, 6)

    def own_rows():
        wait_bytes(trecv, recv_sem.at[5])
        wait_bytes(r_recv, recv_sem.at[6])
        for copy in loads[5:7]:
            copy.wait()
        for n in range(KEPT):
            at = idx(SHARDS * CAP + n)
            gl, gr = unfold(trecv[at])
            turned = unfold(r_recv[pl.ds(at, 1)])[0]
            new_avg[n] = (BETA_ONE * avg[n].astype(jnp.float32) + (1.0 - BETA_ONE) * turned).astype(jnp.bfloat16)
            new_avg_sq[n] = BETA_TWO * avg_sq[n] + (1.0 - BETA_TWO) * turned * turned
            new_left[n] = BETA_TWO * left_gram[n] + (1.0 - BETA_TWO) * gl
            new_right[n] = BETA_TWO * right_gram[n] + (1.0 - BETA_TWO) * gr

    order = [(z_step, 0, m) for m in range(PARTS)]
    for m in range(PARTS):
        order += [(z_step, 1, m), (y_step, 0, m, 1)]
    order += [(y_step, 1, m, 1) for m in range(PARTS)]
    for d in (2, 3, 4):
        order += [(y_step, c, m, d) for c in range(2) for m in range(PARTS)]
    for count, (step, *args) in enumerate(order[:-2]):
        step(*args)
        if count == PARTS - 1:
            send_r()
            pl.when(is_hub)(grams_to_owners)
        if count == 4 * PARTS:
            to_owners()
        if count == len(order) - 4:
            own_rows()

    for copy in pending:
        copy.wait_send()
    for n, ref in ((0, bases_out), (1, moments_out), (5, tsend), (6, r_send)):
        wait_bytes(ref.at[pl.ds(0, CAP * (SHARDS - 1))], send_sem.at[n])

    @pl.when(is_hub)
    def _():
        wait_bytes(bases_row.at[pl.ds(0, KEPT - 1)], send_sem.at[2])
        wait_bytes(moments_row.at[pl.ds(0, KEPT - 1)], send_sem.at[3])
        wait_bytes(rsend.at[pl.ds(0, REPS - 1)], send_sem.at[4])
        for n in range(3 * PARTS):
            wait_bytes(region(0, bits[0], parts[n // 3]), z_send.at[n])

    @pl.when(jnp.logical_not(is_hub))
    def _():
        wait_bytes(bases_row, send_sem.at[2])
        wait_bytes(moments_row, send_sem.at[3])

    for step, *args in order[-2:]:
        step(*args)


def store_kernel(*refs):
    count = len(refs) // 2
    sems = refs[-1]
    copies = []
    for n in range(count):
        src, dst = refs[n], refs[count + n]
        if n == 0:
            for b in range(KEPT):
                i, j = b // 8, b % 8
                place = dst.at[i * W : (i + 1) * W, j * W : (j + 1) * W]
                copies.append(pltpu.make_async_copy(src.at[b], place, sems.at[len(copies)]))
        else:
            copies.append(pltpu.make_async_copy(src, dst, sems.at[len(copies)]))
    for copy in copies:
        copy.start()
    for copy in copies:
        copy.wait()


def body(grad, owner, left_basis, right_basis, avg, avg_sq, left_gram, right_gram):
    vmem = pl.BlockSpec(memory_space=pltpu.VMEM)
    hbm = pl.BlockSpec(memory_space=pltpu.HBM)
    bf16, f32 = jnp.bfloat16, jnp.float32
    slots = SHARDS * CAP
    rows = (KEPT, 8, W)
    outs = [jax.ShapeDtypeStruct(x.shape, x.dtype) for x in (grad, avg, avg_sq, left_gram, right_gram)]
    operands = [
        pltpu.with_memory_space_constraint(x, pltpu.HBM)
        for x in (owner.T, left_basis, right_basis, avg, avg_sq, grad, left_gram, right_gram)
    ]
    results = pl.pallas_call(
        kernel,
        out_shape=[jax.ShapeDtypeStruct((KEPT, W, W), bf16)] + outs[1:],
        in_specs=[hbm] * 8,
        out_specs=[vmem] * 5,
        scratch_shapes=[
            pltpu.VMEM(owner.shape[::-1], jnp.int32),
            pltpu.VMEM((8, 128), jnp.int32),
            pltpu.SMEM((8, 128), jnp.int32),
            pltpu.VMEM(rows, bf16),
            pltpu.VMEM(rows, bf16),
            pltpu.VMEM(rows, bf16),
            pltpu.VMEM(rows, f32),
            pltpu.VMEM(grad.shape, bf16),
            pltpu.VMEM(rows, f32),
            pltpu.VMEM(rows, f32),
            pltpu.VMEM((KEPT, 2, PR, PC), bf16),
            pltpu.VMEM((slots, 2, PR, PC), bf16),
            pltpu.VMEM((slots, 2, PR, PC), bf16),
            pltpu.VMEM((slots, 2, PR, PC), bf16),
            pltpu.VMEM((slots, 2, PR, PC), bf16),
            pltpu.VMEM((KEPT, 2, PR, PC), bf16),
            pltpu.VMEM((KEPT, 2, PR, PC), bf16),
            pltpu.VMEM((REPS, 2, PR, PC), bf16),
            pltpu.VMEM((REPS, 2, PR, PC), bf16),
            pltpu.VMEM((REPS, PR, PC), bf16),
            pltpu.VMEM((KEPT, PR, PC), bf16),
            pltpu.VMEM((KEPT, 2, PR, PC), bf16),
            pltpu.VMEM((slots, 2, PR, PC), bf16),
            pltpu.VMEM((slots, 2, PR, PC), bf16),
            pltpu.VMEM((slots, PR, PC), bf16),
            pltpu.VMEM((slots, PR, PC), bf16),
            pltpu.SemaphoreType.DMA((8,)),
            pltpu.SemaphoreType.DMA,
            pltpu.SemaphoreType.DMA((7,)),
            pltpu.SemaphoreType.DMA((7,)),
            pltpu.SemaphoreType.DMA((3 * PARTS,)),
            pltpu.SemaphoreType.DMA((18 * PARTS,)),
            pltpu.SemaphoreType.DMA((18 * PARTS,)),
        ],
        compiler_params=pltpu.CompilerParams(
            collective_id=0, has_side_effects=True, vmem_limit_bytes=40 * 1024 * 1024
        ),
        cost_estimate=pl.CostEstimate(flops=12 * W**3, bytes_accessed=6 << 20, transcendentals=0),
        name="soap_step",
    )(*operands)
    return tuple(
        pl.pallas_call(
            store_kernel,
            out_shape=outs,
            in_specs=[pl.BlockSpec(memory_space=pl.ANY)] * 5,
            out_specs=[hbm] * 5,
            scratch_shapes=[pltpu.SemaphoreType.DMA((KEPT + 4,))],
            compiler_params=pltpu.CompilerParams(vmem_limit_bytes=4 * 1024 * 1024),
            cost_estimate=pl.CostEstimate(flops=0, bytes_accessed=5 << 20, transcendentals=0),
            name="store",
        )(*results)
    )


def solution(mesh):
    rows = P("shard", "rep", None)
    return jax.shard_map(
        body,
        mesh=mesh,
        in_specs=(P("shard", None), P(), rows, rows, rows, rows, rows, rows),
        out_specs=(P("shard", None), rows, rows, rows, rows),
        check_vma=False,
    )
```

```python
import functools

import jax
import jax.numpy as jnp
from jax import lax
from jax.experimental import pallas as pl
from jax.experimental.pallas import tpu as pltpu
from jax.sharding import PartitionSpec as P

CAP = 2
BETA_ONE = 0.9
BETA_TWO = 0.95
EPSILON = 1e-08

YS = 8
ZS = 4
REPS = YS * ZS
SHARDS = 16
KEPT = 16
W = 256
PR, PC = 16, 128
PARTS = 2
FAR_Y = (4, 3, 5, 2, 6, 1, 7, 0)
FAR_Z = (2, 1, 3, 0)
MESH = pl.DeviceIdType.MESH


def routing(owner_t, here):
    i32, f32 = jnp.int32, jnp.float32
    count = owner_t.shape[0] * owner_t.shape[1]
    cols, rows = owner_t.shape
    square = lax.broadcasted_iota(i32, (rows, rows), 0) == lax.broadcasted_iota(i32, (rows, rows), 1)

    def total(mask, value, axis):
        return jnp.sum(jnp.where(mask, value, 0).astype(f32), axis=axis, keepdims=True).astype(i32)

    def numbers(shape, axis):
        at = lax.broadcasted_iota(i32, shape, axis)
        return at % rows * cols + at // rows, at % rows * cols // KEPT

    flat = jnp.concatenate([total(square, owner_t[j : j + 1, :], 1) for j in range(cols)], axis=0)
    ident, source = numbers((count, 1), 0)
    ident_r, source_r = numbers((1, count), 1)
    diagonal = ident == ident_r
    flat_r = total(diagonal, flat, 0)
    same = (flat == flat_r) & (ident_r < ident)
    rank = total(same, 1, 1)
    pair = total(same & (source == source_r), 1, 1)
    to_slot, from_slot = flat * CAP + pair, source * CAP + pair
    lane = lax.broadcasted_iota(i32, (1, 128), 1)
    slots = SHARDS * CAP
    owned = flat == here
    picked = jnp.where(
        lane < slots,
        jnp.where((source == here) & (to_slot == lane), ident - here * KEPT, 0),
        jnp.where(
            lane < slots + KEPT,
            jnp.where(owned & (rank == lane - slots), from_slot, 0),
            jnp.where(
                lane < 2 * slots + KEPT,
                jnp.where(owned & (from_slot == lane - slots - KEPT), rank, 0),
                jnp.where(ident == here * KEPT + lane - 2 * slots - KEPT, to_slot, 0),
            ),
        ),
    )
    row = jnp.sum(picked.astype(f32), axis=0, keepdims=True).astype(i32)
    of_slots = ((lane >= slots) & (lane < slots + KEPT)) | (lane >= 2 * slots + KEPT)
    row = jnp.maximum(jnp.minimum(row, jnp.where(of_slots, slots - 1, KEPT - 1)), 0)
    return jnp.broadcast_to(row, (8, 128))


def fold(x):
    x = x.astype(jnp.float32)
    return jnp.concatenate([x[:, :, :PC], x[:, :, PC:]], axis=1).astype(jnp.bfloat16)


def unfold(x):
    x = x.astype(jnp.float32)
    return jnp.concatenate([x[:, :8, :], x[:, 8:, :]], axis=2)


def nn(a, b):
    return lax.dot_general(a, b, (((1,), (0,)), ((), ())), preferred_element_type=jnp.float32)


def nt(a, b):
    return lax.dot_general(a, b, (((1,), (1,)), ((), ())), preferred_element_type=jnp.float32)


def tn(a, b):
    return lax.dot_general(a, b, (((0,), (0,)), ((), ())), preferred_element_type=jnp.float32)


def wait_bytes(ref, sem):
    pltpu.make_async_copy(ref, ref, sem).wait()


def kernel(
    owner_h, left_h, right_h, avg_h, avg_sq_h, grad, left_gram_h, right_gram_h,
    update, new_avg, new_avg_sq, new_left, new_right,
    owner, table_v, table, left, right, avg, avg_sq, whole, left_gram, right_gram,
    folded, bases_out, moments_out, bases_in, moments_in, bases_row, moments_row, bases, moments,
    rsend, rbuf, grams, tsend, trecv, r_send, r_recv,
    load_sem, table_sem, send_sem, recv_sem, z_send, ag_send, ag_recv,
):
    r = lax.axis_index("rep")
    s = lax.axis_index("shard")
    y, z = r // ZS, r % ZS
    z_half, z_odd = z // 2, z % 2
    p0 = (y + s) % 2
    is_hub = z_odd == p0

    def wrap(v, n):
        return jnp.where(v >= n, v - n, v)

    ys = [wrap(y + t, YS) for t in range(YS)]
    zs = [wrap(z + t, ZS) for t in range(ZS)]
    z_low, x, core = s // 8, s % 8 // 2, s % 2
    xs = [wrap(x + t, 4) for t in range(4)]
    ss = [
        (1 - z_low if a else z_low) * 8 + xs[b] * 2 + (1 - core if c else core)
        for a, b, c in (
            (1, 2, 1), (1, 2, 0), (0, 2, 1), (0, 2, 0), (1, 1, 1), (1, 1, 0), (1, 3, 1), (1, 3, 0),
            (0, 1, 1), (0, 1, 0), (0, 3, 1), (0, 3, 0), (1, 0, 1), (1, 0, 0), (0, 0, 1),
        )
    ]

    def to(rep):
        return dict(device_id={"rep": rep}, device_id_type=MESH)

    def over(shard):
        return dict(device_id={"shard": shard}, device_id_type=MESH)

    loads = [
        pltpu.make_async_copy(src, dst, load_sem.at[n])
        for n, (src, dst) in enumerate(
            [(left_h, left), (right_h, right), (avg_h, avg), (avg_sq_h, avg_sq),
             (grad, whole), (left_gram_h, left_gram), (right_gram_h, right_gram), (owner_h, owner)]
        )
    ]
    for copy in (loads[7], *loads[:4]):
        copy.start()

    def idx(n):
        return table[0, n]

    barrier = pltpu.get_barrier_semaphore()
    for peer in ss:
        pl.semaphore_signal(barrier, inc=1, **over(peer))

    @pl.when(is_hub)
    def _():
        for t in FAR_Y:
            for v in FAR_Z:
                if t or v:
                    pl.semaphore_signal(barrier, inc=1, **to(ys[t] * ZS + zs[v]))

    loads[7].wait()
    table_v[...] = routing(owner[...], s)
    pltpu.make_async_copy(table_v, table, table_sem).start()

    def pack(first, refs, out):
        for n, ref in enumerate(refs):
            loads[first + n].wait()
            folded[:, n] = fold(ref[...])
        if first == 0:
            pltpu.make_async_copy(table_v, table, table_sem).wait()
        for n in range(SHARDS * CAP):
            out[n] = folded[idx(SHARDS * CAP + KEPT + n)]

    pack(0, (left, right), bases_out)
    pl.semaphore_wait(barrier, jnp.where(is_hub, SHARDS - 1 + KEPT - 1, SHARDS - 1 + KEPT))

    mine = pl.ds(s * CAP, CAP)

    def exchange(src, dst, n):
        pltpu.make_async_copy(src.at[mine], dst.at[mine], recv_sem.at[n]).start()
        for peer in ss:
            pltpu.make_async_remote_copy(
                src.at[pl.ds(peer * CAP, CAP)], dst.at[mine], send_sem.at[n], recv_sem.at[n], **over(peer)
            ).start()

    exchange(bases_out, bases_in, 0)
    pack(2, (avg, avg_sq), moments_out)
    exchange(moments_out, moments_in, 1)
    for copy in loads[4:7]:
        copy.start()

    strip_at = pl.multiple_of(PR * (2 * y + z_half), PR)
    picks = (
        lax.broadcasted_iota(jnp.int32, (PR, W), 1)
        == lax.broadcasted_iota(jnp.int32, (PR, W), 0) + strip_at
    ).astype(jnp.float32).astype(jnp.bfloat16)

    def gram_rows(blocks):
        for b in blocks:
            i, j = b // 8, b % 8
            g = whole[i * W : (i + 1) * W, j * W : (j + 1) * W]
            strip = whole[pl.ds(i * W + strip_at, PR), j * W : (j + 1) * W]
            both = nt(jnp.concatenate([strip, picks], axis=0), g)
            wide = nn(both[PR:].astype(jnp.bfloat16), g)
            for n, v in enumerate((both[:PR], wide)):
                v = jnp.where(z_odd == 1, v[8:], v[:8])
                grams[b, n] = jnp.concatenate([v[:, :PC], v[:, PC:]], axis=0).astype(jnp.bfloat16)

    def to_hub(src, dst, n):
        for t in FAR_Y:
            p = p0 if t % 2 == 0 else 1 - p0
            for b in (1 - z_half, z_half):
                block, h = 2 * ys[t] + b, ys[t] * ZS + 2 * b + p

                def remote(block=block, h=h):
                    pltpu.make_async_remote_copy(
                        src.at[block], dst.at[r], send_sem.at[n], recv_sem.at[n], **to(h)
                    ).start()

                if t == 0:
                    pl.when(h != r)(remote)

                    @pl.when(h == r)
                    def _(block=block):
                        pltpu.make_async_copy(src.at[block], dst.at[r], recv_sem.at[n]).start()
                else:
                    remote()

    loads[4].wait()
    gram_rows(range(0, 4))
    for n, (got, row, out) in enumerate(
        ((bases_in, bases_row, bases), (moments_in, moments_row, moments))
    ):
        wait_bytes(got, recv_sem.at[n])
        for b in range(KEPT):
            row[b] = got[idx(2 * SHARDS * CAP + KEPT + b)]
        to_hub(row, out, 2 + n)
        if n == 0:
            gram_rows(range(4, 9))

    def grams_to_owners():
        gram_rows(range(9, KEPT))
        for m in range(SHARDS * CAP):
            tsend[m] = grams[idx(m)]
        exchange(tsend, trecv, 5)

    pl.when(jnp.logical_not(is_hub))(grams_to_owners)

    block_me = 2 * y + z_half

    @pl.when(is_hub)
    def _():
        g = whole[
            pl.ds(pl.multiple_of(y // 4 * W, W), W),
            pl.ds(pl.multiple_of(y % 4 * (2 * W) + z_half * W, W), W),
        ]
        wait_bytes(bases, recv_sem.at[2])
        lb = unfold(bases[:, 0]).reshape(W, W).astype(jnp.bfloat16)
        rb = unfold(bases[:, 1]).reshape(W, W).astype(jnp.bfloat16)
        half = nn(lb, g).astype(jnp.bfloat16)
        turned = nn(half, rb)
        wait_bytes(moments, recv_sem.at[3])
        m0 = unfold(moments[:, 0]).reshape(W, W)
        v0 = unfold(moments[:, 1]).reshape(W, W)
        first = BETA_ONE * m0 + (1.0 - BETA_ONE) * turned
        second = BETA_TWO * v0 + (1.0 - BETA_TWO) * turned * turned
        scaled = (first / (jnp.sqrt(second) + EPSILON)).astype(jnp.bfloat16)
        back = nt(scaled, rb).astype(jnp.bfloat16)
        update[block_me] = tn(lb, back).astype(jnp.bfloat16)
        rsend[...] = fold(turned.reshape(REPS, 8, W))

    ups = (ys[1] * ZS + z, ys[7] * ZS + z)
    z_pair = 2 * z_half + 1 - z_odd
    z_next = jnp.where(z_odd == 1, zs[1], zs[3])
    pending = []
    names = {}

    def region(t, bit, rows):
        return update.at[2 * ys[t] + bit, pl.ds(rows[0], rows[1] - rows[0])]

    def push(ref, peer, key):
        n = names.setdefault(key, len(names))
        copy = pltpu.make_async_remote_copy(ref, ref, ag_send.at[n], ag_recv.at[n], **to(peer))
        copy.start()
        return copy

    def pull(ref, key):
        wait_bytes(ref, ag_recv.at[names[key]])

    bits = (z_half, 1 - z_half)
    parts = [(n * W // PARTS, (n + 1) * W // PARTS) for n in range(PARTS)]

    @pl.when(is_hub)
    def _():
        for m, rows in enumerate(parts):
            ref = region(0, bits[0], rows)
            for n, (c, peer) in enumerate(((1, zs[2]), (1, z_next), (0, z_pair))):
                key = names.setdefault(("z", c, m), len(names))
                pltpu.make_async_remote_copy(
                    ref, ref, z_send.at[3 * m + n], ag_recv.at[key], **to(y * ZS + peer)
                ).start()

    def y_rows(m, d, way):
        lo, hi = parts[m]
        if d < YS // 2:
            return lo, hi
        mid = (lo + hi) // 2
        return (lo, mid) if way == 0 else (mid, hi)

    def far(d, way):
        return (-d if way == 0 else d) % YS

    def y_push(c, m, d, way):
        ref = region(far(d - 1, way), bits[c], y_rows(m, d, way))
        pending.append(push(ref, ups[way], ("y", c, m, d, way)))

    def z_step(c, m):
        ref = region(0, bits[c], parts[m])
        if c == 0:
            pl.when(jnp.logical_not(is_hub))(lambda: pull(ref, ("z", c, m)))
        else:
            pull(ref, ("z", c, m))
        for way in range(2):
            y_push(c, m, 1, way)

    def y_step(c, m, d):
        for way in range(2):
            pull(region(far(d, way), bits[c], y_rows(m, d, way)), ("y", c, m, d, way))
            if d < YS // 2:
                y_push(c, m, d + 1, way)

    def send_r():
        @pl.when(is_hub)
        def _():
            for t in FAR_Y:
                for v in FAR_Z:
                    q = ys[t] * ZS + zs[v]
                    if t or v:
                        pltpu.make_async_remote_copy(
                            rsend.at[q], rbuf.at[block_me], send_sem.at[4], recv_sem.at[4], **to(q)
                        ).start()
                    else:
                        pltpu.make_async_copy(rsend.at[r], rbuf.at[block_me], recv_sem.at[4]).start()

    def to_owners():
        wait_bytes(rbuf, recv_sem.at[4])
        for m in range(SHARDS * CAP):
            r_send[m] = rbuf[idx(m)]
        exchange(r_send, r_recv, 6)

    def own_rows():
        wait_bytes(trecv, recv_sem.at[5])
        wait_bytes(r_recv, recv_sem.at[6])
        for copy in loads[5:7]:
            copy.wait()
        for n in range(KEPT):
            at = idx(SHARDS * CAP + n)
            gl, gr = unfold(trecv[at])
            turned = unfold(r_recv[pl.ds(at, 1)])[0]
            new_avg[n] = (BETA_ONE * avg[n].astype(jnp.float32) + (1.0 - BETA_ONE) * turned).astype(jnp.bfloat16)
            new_avg_sq[n] = BETA_TWO * avg_sq[n] + (1.0 - BETA_TWO) * turned * turned
            new_left[n] = BETA_TWO * left_gram[n] + (1.0 - BETA_TWO) * gl
            new_right[n] = BETA_TWO * right_gram[n] + (1.0 - BETA_TWO) * gr

    order = [(z_step, 0, m) for m in range(PARTS)]
    for m in range(PARTS):
        order += [(z_step, 1, m), (y_step, 0, m, 1)]
    for c, d in ((0, 2), (1, 1), (0, 3), (1, 2), (0, 4), (1, 3), (1, 4)):
        order += [(y_step, c, m, d) for m in range(PARTS)]
    for count, (step, *args) in enumerate(order[:-2]):
        step(*args)
        if count == PARTS - 1:
            send_r()
            pl.when(is_hub)(grams_to_owners)
        if count == 4 * PARTS:
            to_owners()
        if count == len(order) - 4:
            own_rows()

    for copy in pending:
        copy.wait_send()
    for n, ref in ((0, bases_out), (1, moments_out), (5, tsend), (6, r_send)):
        wait_bytes(ref.at[pl.ds(0, CAP * (SHARDS - 1))], send_sem.at[n])

    @pl.when(is_hub)
    def _():
        wait_bytes(bases_row.at[pl.ds(0, KEPT - 1)], send_sem.at[2])
        wait_bytes(moments_row.at[pl.ds(0, KEPT - 1)], send_sem.at[3])
        wait_bytes(rsend.at[pl.ds(0, REPS - 1)], send_sem.at[4])
        for n in range(3 * PARTS):
            wait_bytes(region(0, bits[0], parts[n // 3]), z_send.at[n])

    @pl.when(jnp.logical_not(is_hub))
    def _():
        wait_bytes(bases_row, send_sem.at[2])
        wait_bytes(moments_row, send_sem.at[3])

    for step, *args in order[-2:]:
        step(*args)


def store_kernel(*refs):
    count = len(refs) // 2
    sems = refs[-1]
    copies = []
    for n in range(count):
        src, dst = refs[n], refs[count + n]
        if n == 0:
            for b in range(KEPT):
                i, j = b // 8, b % 8
                place = dst.at[i * W : (i + 1) * W, j * W : (j + 1) * W]
                copies.append(pltpu.make_async_copy(src.at[b], place, sems.at[len(copies)]))
        else:
            copies.append(pltpu.make_async_copy(src, dst, sems.at[len(copies)]))
    for copy in copies:
        copy.start()
    for copy in copies:
        copy.wait()


def body(grad, owner, left_basis, right_basis, avg, avg_sq, left_gram, right_gram):
    vmem = pl.BlockSpec(memory_space=pltpu.VMEM)
    hbm = pl.BlockSpec(memory_space=pltpu.HBM)
    bf16, f32 = jnp.bfloat16, jnp.float32
    slots = SHARDS * CAP
    rows = (KEPT, 8, W)
    outs = [jax.ShapeDtypeStruct(x.shape, x.dtype) for x in (grad, avg, avg_sq, left_gram, right_gram)]
    operands = [
        pltpu.with_memory_space_constraint(x, pltpu.HBM)
        for x in (owner.T, left_basis, right_basis, avg, avg_sq, grad, left_gram, right_gram)
    ]
    results = pl.pallas_call(
        kernel,
        out_shape=[jax.ShapeDtypeStruct((KEPT, W, W), bf16)] + outs[1:],
        in_specs=[hbm] * 8,
        out_specs=[vmem] * 5,
        scratch_shapes=[
            pltpu.VMEM(owner.shape[::-1], jnp.int32),
            pltpu.VMEM((8, 128), jnp.int32),
            pltpu.SMEM((8, 128), jnp.int32),
            pltpu.VMEM(rows, bf16),
            pltpu.VMEM(rows, bf16),
            pltpu.VMEM(rows, bf16),
            pltpu.VMEM(rows, f32),
            pltpu.VMEM(grad.shape, bf16),
            pltpu.VMEM(rows, f32),
            pltpu.VMEM(rows, f32),
            pltpu.VMEM((KEPT, 2, PR, PC), bf16),
            pltpu.VMEM((slots, 2, PR, PC), bf16),
            pltpu.VMEM((slots, 2, PR, PC), bf16),
            pltpu.VMEM((slots, 2, PR, PC), bf16),
            pltpu.VMEM((slots, 2, PR, PC), bf16),
            pltpu.VMEM((KEPT, 2, PR, PC), bf16),
            pltpu.VMEM((KEPT, 2, PR, PC), bf16),
            pltpu.VMEM((REPS, 2, PR, PC), bf16),
            pltpu.VMEM((REPS, 2, PR, PC), bf16),
            pltpu.VMEM((REPS, PR, PC), bf16),
            pltpu.VMEM((KEPT, PR, PC), bf16),
            pltpu.VMEM((KEPT, 2, PR, PC), bf16),
            pltpu.VMEM((slots, 2, PR, PC), bf16),
            pltpu.VMEM((slots, 2, PR, PC), bf16),
            pltpu.VMEM((slots, PR, PC), bf16),
            pltpu.VMEM((slots, PR, PC), bf16),
            pltpu.SemaphoreType.DMA((8,)),
            pltpu.SemaphoreType.DMA,
            pltpu.SemaphoreType.DMA((7,)),
            pltpu.SemaphoreType.DMA((7,)),
            pltpu.SemaphoreType.DMA((3 * PARTS,)),
            pltpu.SemaphoreType.DMA((18 * PARTS,)),
            pltpu.SemaphoreType.DMA((18 * PARTS,)),
        ],
        compiler_params=pltpu.CompilerParams(
            collective_id=0, has_side_effects=True, vmem_limit_bytes=40 * 1024 * 1024
        ),
        cost_estimate=pl.CostEstimate(flops=12 * W**3, bytes_accessed=6 << 20, transcendentals=0),
        name="soap_step",
    )(*operands)
    return tuple(
        pl.pallas_call(
            store_kernel,
            out_shape=outs,
            in_specs=[pl.BlockSpec(memory_space=pl.ANY)] * 5,
            out_specs=[hbm] * 5,
            scratch_shapes=[pltpu.SemaphoreType.DMA((KEPT + 4,))],
            compiler_params=pltpu.CompilerParams(vmem_limit_bytes=4 * 1024 * 1024),
            cost_estimate=pl.CostEstimate(flops=0, bytes_accessed=5 << 20, transcendentals=0),
            name="store",
        )(*results)
    )


def solution(mesh):
    rows = P("shard", "rep", None)
    return jax.shard_map(
        body,
        mesh=mesh,
        in_specs=(P("shard", None), P(), rows, rows, rows, rows, rows, rows),
        out_specs=(P("shard", None), rows, rows, rows, rows),
        check_vma=False,
    )
```

```python
import functools

import jax
import jax.numpy as jnp
from jax import lax
from jax.experimental import pallas as pl
from jax.experimental.pallas import tpu as pltpu
from jax.sharding import PartitionSpec as P

CAP = 2
BETA_ONE = 0.9
BETA_TWO = 0.95
EPSILON = 1e-08

YS = 8
ZS = 4
REPS = YS * ZS
SHARDS = 16
KEPT = 16
W = 256
PR, PC = 16, 128
PARTS = 4
FAR_Y = (4, 3, 5, 2, 6, 1, 7, 0)
FAR_Z = (2, 1, 3, 0)
MESH = pl.DeviceIdType.MESH


def routing(owner_t, here):
    i32, f32 = jnp.int32, jnp.float32
    count = owner_t.shape[0] * owner_t.shape[1]
    cols, rows = owner_t.shape
    square = lax.broadcasted_iota(i32, (rows, rows), 0) == lax.broadcasted_iota(i32, (rows, rows), 1)

    def total(mask, value, axis):
        return jnp.sum(jnp.where(mask, value, 0).astype(f32), axis=axis, keepdims=True).astype(i32)

    def numbers(shape, axis):
        at = lax.broadcasted_iota(i32, shape, axis)
        return at % rows * cols + at // rows, at % rows * cols // KEPT

    flat = jnp.concatenate([total(square, owner_t[j : j + 1, :], 1) for j in range(cols)], axis=0)
    ident, source = numbers((count, 1), 0)
    ident_r, source_r = numbers((1, count), 1)
    diagonal = ident == ident_r
    flat_r = total(diagonal, flat, 0)
    same = (flat == flat_r) & (ident_r < ident)
    rank = total(same, 1, 1)
    pair = total(same & (source == source_r), 1, 1)
    to_slot, from_slot = flat * CAP + pair, source * CAP + pair
    lane = lax.broadcasted_iota(i32, (1, 128), 1)
    slots = SHARDS * CAP
    owned = flat == here
    picked = jnp.where(
        lane < slots,
        jnp.where((source == here) & (to_slot == lane), ident - here * KEPT, 0),
        jnp.where(
            lane < slots + KEPT,
            jnp.where(owned & (rank == lane - slots), from_slot, 0),
            jnp.where(
                lane < 2 * slots + KEPT,
                jnp.where(owned & (from_slot == lane - slots - KEPT), rank, 0),
                jnp.where(ident == here * KEPT + lane - 2 * slots - KEPT, to_slot, 0),
            ),
        ),
    )
    row = jnp.sum(picked.astype(f32), axis=0, keepdims=True).astype(i32)
    of_slots = ((lane >= slots) & (lane < slots + KEPT)) | (lane >= 2 * slots + KEPT)
    row = jnp.maximum(jnp.minimum(row, jnp.where(of_slots, slots - 1, KEPT - 1)), 0)
    return jnp.broadcast_to(row, (8, 128))


def fold(x):
    x = x.astype(jnp.float32)
    return jnp.concatenate([x[:, :, :PC], x[:, :, PC:]], axis=1).astype(jnp.bfloat16)


def unfold(x):
    x = x.astype(jnp.float32)
    return jnp.concatenate([x[:, :8, :], x[:, 8:, :]], axis=2)


def nn(a, b):
    return lax.dot_general(a, b, (((1,), (0,)), ((), ())), preferred_element_type=jnp.float32)


def nt(a, b):
    return lax.dot_general(a, b, (((1,), (1,)), ((), ())), preferred_element_type=jnp.float32)


def tn(a, b):
    return lax.dot_general(a, b, (((0,), (0,)), ((), ())), preferred_element_type=jnp.float32)


def wait_bytes(ref, sem):
    pltpu.make_async_copy(ref, ref, sem).wait()


def kernel(
    owner_h, left_h, right_h, avg_h, avg_sq_h, grad, left_gram_h, right_gram_h,
    update, new_avg, new_avg_sq, new_left, new_right,
    owner, table_v, table, left, right, avg, avg_sq, whole, left_gram, right_gram,
    folded, bases_out, moments_out, bases_in, moments_in, bases_row, moments_row, bases, moments,
    rsend, rbuf, grams, tsend, trecv, r_send, r_recv,
    load_sem, table_sem, send_sem, recv_sem, z_send, ag_send, ag_recv,
):
    r = lax.axis_index("rep")
    s = lax.axis_index("shard")
    y, z = r // ZS, r % ZS
    z_half, z_odd = z // 2, z % 2
    p0 = (y + s) % 2
    is_hub = z_odd == p0

    def wrap(v, n):
        return jnp.where(v >= n, v - n, v)

    ys = [wrap(y + t, YS) for t in range(YS)]
    zs = [wrap(z + t, ZS) for t in range(ZS)]
    z_low, x, core = s // 8, s % 8 // 2, s % 2
    xs = [wrap(x + t, 4) for t in range(4)]
    ss = [
        (1 - z_low if a else z_low) * 8 + xs[b] * 2 + (1 - core if c else core)
        for a, b, c in (
            (1, 2, 1), (1, 2, 0), (0, 2, 1), (0, 2, 0), (1, 1, 1), (1, 1, 0), (1, 3, 1), (1, 3, 0),
            (0, 1, 1), (0, 1, 0), (0, 3, 1), (0, 3, 0), (1, 0, 1), (1, 0, 0), (0, 0, 1),
        )
    ]

    def to(rep):
        return dict(device_id={"rep": rep}, device_id_type=MESH)

    def over(shard):
        return dict(device_id={"shard": shard}, device_id_type=MESH)

    loads = [
        pltpu.make_async_copy(src, dst, load_sem.at[n])
        for n, (src, dst) in enumerate(
            [(left_h, left), (right_h, right), (avg_h, avg), (avg_sq_h, avg_sq),
             (grad, whole), (left_gram_h, left_gram), (right_gram_h, right_gram), (owner_h, owner)]
        )
    ]
    for copy in (loads[7], *loads[:4]):
        copy.start()

    def idx(n):
        return table[0, n]

    barrier = pltpu.get_barrier_semaphore()
    for peer in ss:
        pl.semaphore_signal(barrier, inc=1, **over(peer))

    @pl.when(is_hub)
    def _():
        for t in FAR_Y:
            for v in FAR_Z:
                if t or v:
                    pl.semaphore_signal(barrier, inc=1, **to(ys[t] * ZS + zs[v]))

    loads[7].wait()
    table_v[...] = routing(owner[...], s)
    pltpu.make_async_copy(table_v, table, table_sem).start()

    def pack(first, refs, out):
        for n, ref in enumerate(refs):
            loads[first + n].wait()
            folded[:, n] = fold(ref[...])
        if first == 0:
            pltpu.make_async_copy(table_v, table, table_sem).wait()
        for n in range(SHARDS * CAP):
            out[n] = folded[idx(SHARDS * CAP + KEPT + n)]

    pack(0, (left, right), bases_out)
    pl.semaphore_wait(barrier, jnp.where(is_hub, SHARDS - 1 + KEPT - 1, SHARDS - 1 + KEPT))

    mine = pl.ds(s * CAP, CAP)

    def exchange(src, dst, n):
        pltpu.make_async_copy(src.at[mine], dst.at[mine], recv_sem.at[n]).start()
        for peer in ss:
            pltpu.make_async_remote_copy(
                src.at[pl.ds(peer * CAP, CAP)], dst.at[mine], send_sem.at[n], recv_sem.at[n], **over(peer)
            ).start()

    exchange(bases_out, bases_in, 0)
    pack(2, (avg, avg_sq), moments_out)
    exchange(moments_out, moments_in, 1)
    for copy in loads[4:7]:
        copy.start()

    strip_at = pl.multiple_of(PR * (2 * y + z_half), PR)
    picks = (
        lax.broadcasted_iota(jnp.int32, (PR, W), 1)
        == lax.broadcasted_iota(jnp.int32, (PR, W), 0) + strip_at
    ).astype(jnp.float32).astype(jnp.bfloat16)

    def gram_rows(blocks):
        for b in blocks:
            i, j = b // 8, b % 8
            g = whole[i * W : (i + 1) * W, j * W : (j + 1) * W]
            strip = whole[pl.ds(i * W + strip_at, PR), j * W : (j + 1) * W]
            both = nt(jnp.concatenate([strip, picks], axis=0), g)
            wide = nn(both[PR:].astype(jnp.bfloat16), g)
            for n, v in enumerate((both[:PR], wide)):
                v = jnp.where(z_odd == 1, v[8:], v[:8])
                grams[b, n] = jnp.concatenate([v[:, :PC], v[:, PC:]], axis=0).astype(jnp.bfloat16)

    def to_hub(src, dst, n):
        for t in FAR_Y:
            p = p0 if t % 2 == 0 else 1 - p0
            for b in (1 - z_half, z_half):
                block, h = 2 * ys[t] + b, ys[t] * ZS + 2 * b + p

                def remote(block=block, h=h):
                    pltpu.make_async_remote_copy(
                        src.at[block], dst.at[r], send_sem.at[n], recv_sem.at[n], **to(h)
                    ).start()

                if t == 0:
                    pl.when(h != r)(remote)

                    @pl.when(h == r)
                    def _(block=block):
                        pltpu.make_async_copy(src.at[block], dst.at[r], recv_sem.at[n]).start()
                else:
                    remote()

    loads[4].wait()
    gram_rows(range(0, 4))
    for n, (got, row, out) in enumerate(
        ((bases_in, bases_row, bases), (moments_in, moments_row, moments))
    ):
        wait_bytes(got, recv_sem.at[n])
        for b in range(KEPT):
            row[b] = got[idx(2 * SHARDS * CAP + KEPT + b)]
        to_hub(row, out, 2 + n)
        if n == 0:
            gram_rows(range(4, 9))

    def grams_to_owners():
        gram_rows(range(9, KEPT))
        for m in range(SHARDS * CAP):
            tsend[m] = grams[idx(m)]
        exchange(tsend, trecv, 5)

    pl.when(jnp.logical_not(is_hub))(grams_to_owners)

    block_me = 2 * y + z_half

    @pl.when(is_hub)
    def _():
        g = whole[
            pl.ds(pl.multiple_of(y // 4 * W, W), W),
            pl.ds(pl.multiple_of(y % 4 * (2 * W) + z_half * W, W), W),
        ]
        wait_bytes(bases, recv_sem.at[2])
        lb = unfold(bases[:, 0]).reshape(W, W).astype(jnp.bfloat16)
        rb = unfold(bases[:, 1]).reshape(W, W).astype(jnp.bfloat16)
        half = nn(lb, g).astype(jnp.bfloat16)
        turned = nn(half, rb)
        wait_bytes(moments, recv_sem.at[3])
        m0 = unfold(moments[:, 0]).reshape(W, W)
        v0 = unfold(moments[:, 1]).reshape(W, W)
        first = BETA_ONE * m0 + (1.0 - BETA_ONE) * turned
        second = BETA_TWO * v0 + (1.0 - BETA_TWO) * turned * turned
        scaled = (first / (jnp.sqrt(second) + EPSILON)).astype(jnp.bfloat16)
        back = nt(scaled, rb).astype(jnp.bfloat16)
        update[block_me] = tn(lb, back).astype(jnp.bfloat16)
        rsend[...] = fold(turned.reshape(REPS, 8, W))

    ups = (ys[1] * ZS + z, ys[7] * ZS + z)
    z_pair = 2 * z_half + 1 - z_odd
    z_next = jnp.where(z_odd == 1, zs[1], zs[3])
    pending = []
    names = {}

    def region(t, bit, rows):
        return update.at[2 * ys[t] + bit, pl.ds(rows[0], rows[1] - rows[0])]

    def push(ref, peer, key):
        n = names.setdefault(key, len(names))
        copy = pltpu.make_async_remote_copy(ref, ref, ag_send.at[n], ag_recv.at[n], **to(peer))
        copy.start()
        return copy

    def pull(ref, key):
        wait_bytes(ref, ag_recv.at[names[key]])

    bits = (z_half, 1 - z_half)
    parts = [(n * W // PARTS, (n + 1) * W // PARTS) for n in range(PARTS)]

    @pl.when(is_hub)
    def _():
        for m, rows in enumerate(parts):
            ref = region(0, bits[0], rows)
            for n, (c, peer) in enumerate(((1, zs[2]), (1, z_next), (0, z_pair))):
                key = names.setdefault(("z", c, m), len(names))
                pltpu.make_async_remote_copy(
                    ref, ref, z_send.at[3 * m + n], ag_recv.at[key], **to(y * ZS + peer)
                ).start()

    def y_rows(m, d, way):
        lo, hi = parts[m]
        if d < YS // 2:
            return lo, hi
        mid = (lo + hi) // 2
        return (lo, mid) if way == 0 else (mid, hi)

    def far(d, way):
        return (-d if way == 0 else d) % YS

    def y_push(c, m, d, way):
        ref = region(far(d - 1, way), bits[c], y_rows(m, d, way))
        pending.append(push(ref, ups[way], ("y", c, m, d, way)))

    def z_step(c, m):
        ref = region(0, bits[c], parts[m])
        if c == 0:
            pl.when(jnp.logical_not(is_hub))(lambda: pull(ref, ("z", c, m)))
        else:
            pull(ref, ("z", c, m))
        for way in range(2):
            y_push(c, m, 1, way)

    def y_step(c, m, d):
        for way in range(2):
            pull(region(far(d, way), bits[c], y_rows(m, d, way)), ("y", c, m, d, way))
            if d < YS // 2:
                y_push(c, m, d + 1, way)

    def send_r():
        @pl.when(is_hub)
        def _():
            for t in FAR_Y:
                for v in FAR_Z:
                    q = ys[t] * ZS + zs[v]
                    if t or v:
                        pltpu.make_async_remote_copy(
                            rsend.at[q], rbuf.at[block_me], send_sem.at[4], recv_sem.at[4], **to(q)
                        ).start()
                    else:
                        pltpu.make_async_copy(rsend.at[r], rbuf.at[block_me], recv_sem.at[4]).start()

    def to_owners():
        wait_bytes(rbuf, recv_sem.at[4])
        for m in range(SHARDS * CAP):
            r_send[m] = rbuf[idx(m)]
        exchange(r_send, r_recv, 6)

    def own_rows():
        wait_bytes(trecv, recv_sem.at[5])
        wait_bytes(r_recv, recv_sem.at[6])
        for copy in loads[5:7]:
            copy.wait()
        for n in range(KEPT):
            at = idx(SHARDS * CAP + n)
            gl, gr = unfold(trecv[at])
            turned = unfold(r_recv[pl.ds(at, 1)])[0]
            new_avg[n] = (BETA_ONE * avg[n].astype(jnp.float32) + (1.0 - BETA_ONE) * turned).astype(jnp.bfloat16)
            new_avg_sq[n] = BETA_TWO * avg_sq[n] + (1.0 - BETA_TWO) * turned * turned
            new_left[n] = BETA_TWO * left_gram[n] + (1.0 - BETA_TWO) * gl
            new_right[n] = BETA_TWO * right_gram[n] + (1.0 - BETA_TWO) * gr

    order = [(z_step, 0, m) for m in range(PARTS)]
    for m in range(PARTS):
        order += [(z_step, 1, m), (y_step, 0, m, 1)]
    order += [(y_step, 1, m, 1) for m in range(PARTS)]
    for d in (2, 3, 4):
        order += [(y_step, c, m, d) for c in range(2) for m in range(PARTS)]
    for count, (step, *args) in enumerate(order[:-2]):
        step(*args)
        if count == PARTS - 1:
            send_r()
            pl.when(is_hub)(grams_to_owners)
        if count == 4 * PARTS:
            to_owners()
        if count == len(order) - 4:
            own_rows()

    for copy in pending:
        copy.wait_send()
    for n, ref in ((0, bases_out), (1, moments_out), (5, tsend), (6, r_send)):
        wait_bytes(ref.at[pl.ds(0, CAP * (SHARDS - 1))], send_sem.at[n])

    @pl.when(is_hub)
    def _():
        wait_bytes(bases_row.at[pl.ds(0, KEPT - 1)], send_sem.at[2])
        wait_bytes(moments_row.at[pl.ds(0, KEPT - 1)], send_sem.at[3])
        wait_bytes(rsend.at[pl.ds(0, REPS - 1)], send_sem.at[4])
        for n in range(3 * PARTS):
            wait_bytes(region(0, bits[0], parts[n // 3]), z_send.at[n])

    @pl.when(jnp.logical_not(is_hub))
    def _():
        wait_bytes(bases_row, send_sem.at[2])
        wait_bytes(moments_row, send_sem.at[3])

    for step, *args in order[-2:]:
        step(*args)


def store_kernel(*refs):
    count = len(refs) // 2
    sems = refs[-1]
    copies = []
    for n in range(count):
        src, dst = refs[n], refs[count + n]
        if n == 0:
            for b in range(KEPT):
                i, j = b // 8, b % 8
                place = dst.at[i * W : (i + 1) * W, j * W : (j + 1) * W]
                copies.append(pltpu.make_async_copy(src.at[b], place, sems.at[len(copies)]))
        else:
            copies.append(pltpu.make_async_copy(src, dst, sems.at[len(copies)]))
    for copy in copies:
        copy.start()
    for copy in copies:
        copy.wait()


def body(grad, owner, left_basis, right_basis, avg, avg_sq, left_gram, right_gram):
    vmem = pl.BlockSpec(memory_space=pltpu.VMEM)
    hbm = pl.BlockSpec(memory_space=pltpu.HBM)
    bf16, f32 = jnp.bfloat16, jnp.float32
    slots = SHARDS * CAP
    rows = (KEPT, 8, W)
    outs = [jax.ShapeDtypeStruct(x.shape, x.dtype) for x in (grad, avg, avg_sq, left_gram, right_gram)]
    operands = [
        pltpu.with_memory_space_constraint(x, pltpu.HBM)
        for x in (owner.T, left_basis, right_basis, avg, avg_sq, grad, left_gram, right_gram)
    ]
    results = pl.pallas_call(
        kernel,
        out_shape=[jax.ShapeDtypeStruct((KEPT, W, W), bf16)] + outs[1:],
        in_specs=[hbm] * 8,
        out_specs=[vmem] * 5,
        scratch_shapes=[
            pltpu.VMEM(owner.shape[::-1], jnp.int32),
            pltpu.VMEM((8, 128), jnp.int32),
            pltpu.SMEM((8, 128), jnp.int32),
            pltpu.VMEM(rows, bf16),
            pltpu.VMEM(rows, bf16),
            pltpu.VMEM(rows, bf16),
            pltpu.VMEM(rows, f32),
            pltpu.VMEM(grad.shape, bf16),
            pltpu.VMEM(rows, f32),
            pltpu.VMEM(rows, f32),
            pltpu.VMEM((KEPT, 2, PR, PC), bf16),
            pltpu.VMEM((slots, 2, PR, PC), bf16),
            pltpu.VMEM((slots, 2, PR, PC), bf16),
            pltpu.VMEM((slots, 2, PR, PC), bf16),
            pltpu.VMEM((slots, 2, PR, PC), bf16),
            pltpu.VMEM((KEPT, 2, PR, PC), bf16),
            pltpu.VMEM((KEPT, 2, PR, PC), bf16),
            pltpu.VMEM((REPS, 2, PR, PC), bf16),
            pltpu.VMEM((REPS, 2, PR, PC), bf16),
            pltpu.VMEM((REPS, PR, PC), bf16),
            pltpu.VMEM((KEPT, PR, PC), bf16),
            pltpu.VMEM((KEPT, 2, PR, PC), bf16),
            pltpu.VMEM((slots, 2, PR, PC), bf16),
            pltpu.VMEM((slots, 2, PR, PC), bf16),
            pltpu.VMEM((slots, PR, PC), bf16),
            pltpu.VMEM((slots, PR, PC), bf16),
            pltpu.SemaphoreType.DMA((8,)),
            pltpu.SemaphoreType.DMA,
            pltpu.SemaphoreType.DMA((7,)),
            pltpu.SemaphoreType.DMA((7,)),
            pltpu.SemaphoreType.DMA((3 * PARTS,)),
            pltpu.SemaphoreType.DMA((18 * PARTS,)),
            pltpu.SemaphoreType.DMA((18 * PARTS,)),
        ],
        compiler_params=pltpu.CompilerParams(
            collective_id=0, has_side_effects=True, vmem_limit_bytes=40 * 1024 * 1024
        ),
        cost_estimate=pl.CostEstimate(flops=12 * W**3, bytes_accessed=6 << 20, transcendentals=0),
        name="soap_step",
    )(*operands)
    return tuple(
        pl.pallas_call(
            store_kernel,
            out_shape=outs,
            in_specs=[pl.BlockSpec(memory_space=pl.ANY)] * 5,
            out_specs=[hbm] * 5,
            scratch_shapes=[pltpu.SemaphoreType.DMA((KEPT + 4,))],
            compiler_params=pltpu.CompilerParams(vmem_limit_bytes=4 * 1024 * 1024),
            cost_estimate=pl.CostEstimate(flops=0, bytes_accessed=5 << 20, transcendentals=0),
            name="store",
        )(*results)
    )


def solution(mesh):
    rows = P("shard", "rep", None)
    return jax.shard_map(
        body,
        mesh=mesh,
        in_specs=(P("shard", None), P(), rows, rows, rows, rows, rows, rows),
        out_specs=(P("shard", None), rows, rows, rows, rows),
        check_vma=False,
    )
```

```python
import functools

import jax
import jax.numpy as jnp
from jax import lax
from jax.experimental import pallas as pl
from jax.experimental.pallas import tpu as pltpu
from jax.sharding import PartitionSpec as P

CAP = 2
BETA_ONE = 0.9
BETA_TWO = 0.95
EPSILON = 1e-08

YS = 8
ZS = 4
REPS = YS * ZS
SHARDS = 16
KEPT = 16
W = 256
PR, PC = 16, 128
PARTS = 2
FAR_Y = (4, 3, 5, 2, 6, 1, 7, 0)
FAR_Z = (2, 1, 3, 0)
MESH = pl.DeviceIdType.MESH


def routing(owner_t, here):
    i32, f32 = jnp.int32, jnp.float32
    count = owner_t.shape[0] * owner_t.shape[1]
    cols, rows = owner_t.shape
    square = lax.broadcasted_iota(i32, (rows, rows), 0) == lax.broadcasted_iota(i32, (rows, rows), 1)

    def total(mask, value, axis):
        return jnp.sum(jnp.where(mask, value, 0).astype(f32), axis=axis, keepdims=True).astype(i32)

    def numbers(shape, axis):
        at = lax.broadcasted_iota(i32, shape, axis)
        return at % rows * cols + at // rows, at % rows * cols // KEPT

    flat = jnp.concatenate([total(square, owner_t[j : j + 1, :], 1) for j in range(cols)], axis=0)
    ident, source = numbers((count, 1), 0)
    ident_r, source_r = numbers((1, count), 1)
    diagonal = ident == ident_r
    flat_r = total(diagonal, flat, 0)
    same = (flat == flat_r) & (ident_r < ident)
    rank = total(same, 1, 1)
    pair = total(same & (source == source_r), 1, 1)
    to_slot, from_slot = flat * CAP + pair, source * CAP + pair
    lane = lax.broadcasted_iota(i32, (1, 128), 1)
    slots = SHARDS * CAP
    owned = flat == here
    picked = jnp.where(
        lane < slots,
        jnp.where((source == here) & (to_slot == lane), ident - here * KEPT, 0),
        jnp.where(
            lane < slots + KEPT,
            jnp.where(owned & (rank == lane - slots), from_slot, 0),
            jnp.where(
                lane < 2 * slots + KEPT,
                jnp.where(owned & (from_slot == lane - slots - KEPT), rank, 0),
                jnp.where(ident == here * KEPT + lane - 2 * slots - KEPT, to_slot, 0),
            ),
        ),
    )
    row = jnp.sum(picked.astype(f32), axis=0, keepdims=True).astype(i32)
    of_slots = ((lane >= slots) & (lane < slots + KEPT)) | (lane >= 2 * slots + KEPT)
    row = jnp.maximum(jnp.minimum(row, jnp.where(of_slots, slots - 1, KEPT - 1)), 0)
    return jnp.broadcast_to(row, (8, 128))


def fold(x):
    x = x.astype(jnp.float32)
    return jnp.concatenate([x[:, :, :PC], x[:, :, PC:]], axis=1).astype(jnp.bfloat16)


def unfold(x):
    x = x.astype(jnp.float32)
    return jnp.concatenate([x[:, :8, :], x[:, 8:, :]], axis=2)


def nn(a, b):
    return lax.dot_general(a, b, (((1,), (0,)), ((), ())), preferred_element_type=jnp.float32)


def nt(a, b):
    return lax.dot_general(a, b, (((1,), (1,)), ((), ())), preferred_element_type=jnp.float32)


def tn(a, b):
    return lax.dot_general(a, b, (((0,), (0,)), ((), ())), preferred_element_type=jnp.float32)


def wait_bytes(ref, sem):
    pltpu.make_async_copy(ref, ref, sem).wait()


def kernel(
    owner_h, left_h, right_h, avg_h, avg_sq_h, grad, left_gram_h, right_gram_h,
    update, new_avg, new_avg_sq, new_left, new_right,
    owner, table_v, table, left, right, avg, avg_sq, whole, left_gram, right_gram,
    folded, bases_out, moments_out, bases_in, moments_in, bases_row, moments_row, bases, moments,
    rsend, rbuf, grams, tsend, trecv, r_send, r_recv,
    load_sem, table_sem, send_sem, recv_sem, z_send, ag_send, ag_recv,
):
    r = lax.axis_index("rep")
    s = lax.axis_index("shard")
    y, z = r // ZS, r % ZS
    z_half, z_odd = z // 2, z % 2
    p0 = (y + s) % 2
    is_hub = z_odd == p0

    def wrap(v, n):
        return jnp.where(v >= n, v - n, v)

    ys = [wrap(y + t, YS) for t in range(YS)]
    zs = [wrap(z + t, ZS) for t in range(ZS)]
    z_low, x, core = s // 8, s % 8 // 2, s % 2
    xs = [wrap(x + t, 4) for t in range(4)]
    ss = [
        (1 - z_low if a else z_low) * 8 + xs[b] * 2 + (1 - core if c else core)
        for a, b, c in (
            (1, 2, 1), (1, 2, 0), (0, 2, 1), (0, 2, 0), (1, 1, 1), (1, 1, 0), (1, 3, 1), (1, 3, 0),
            (0, 1, 1), (0, 1, 0), (0, 3, 1), (0, 3, 0), (1, 0, 1), (1, 0, 0), (0, 0, 1),
        )
    ]

    def to(rep):
        return dict(device_id={"rep": rep}, device_id_type=MESH)

    def over(shard):
        return dict(device_id={"shard": shard}, device_id_type=MESH)

    loads = [
        pltpu.make_async_copy(src, dst, load_sem.at[n])
        for n, (src, dst) in enumerate(
            [(left_h, left), (right_h, right), (avg_h, avg), (avg_sq_h, avg_sq),
             (grad, whole), (left_gram_h, left_gram), (right_gram_h, right_gram), (owner_h, owner)]
        )
    ]
    for copy in (loads[7], *loads[:4]):
        copy.start()

    def idx(n):
        return table[0, n]

    barrier = pltpu.get_barrier_semaphore()
    for peer in ss:
        pl.semaphore_signal(barrier, inc=1, **over(peer))

    @pl.when(is_hub)
    def _():
        for t in FAR_Y:
            for v in FAR_Z:
                if t or v:
                    pl.semaphore_signal(barrier, inc=1, **to(ys[t] * ZS + zs[v]))

    loads[7].wait()
    table_v[...] = routing(owner[...], s)
    pltpu.make_async_copy(table_v, table, table_sem).start()

    def pack(first, refs, out):
        for n, ref in enumerate(refs):
            loads[first + n].wait()
            folded[:, n] = fold(ref[...])
        if first == 0:
            pltpu.make_async_copy(table_v, table, table_sem).wait()
        for n in range(SHARDS * CAP):
            out[n] = folded[idx(SHARDS * CAP + KEPT + n)]

    pack(0, (left, right), bases_out)
    pl.semaphore_wait(barrier, jnp.where(is_hub, SHARDS - 1 + KEPT - 1, SHARDS - 1 + KEPT))

    mine = pl.ds(s * CAP, CAP)

    def exchange(src, dst, n):
        pltpu.make_async_copy(src.at[mine], dst.at[mine], recv_sem.at[n]).start()
        for peer in ss:
            pltpu.make_async_remote_copy(
                src.at[pl.ds(peer * CAP, CAP)], dst.at[mine], send_sem.at[n], recv_sem.at[n], **over(peer)
            ).start()

    exchange(bases_out, bases_in, 0)
    pack(2, (avg, avg_sq), moments_out)
    exchange(moments_out, moments_in, 1)
    for copy in loads[4:7]:
        copy.start()

    strip_at = pl.multiple_of(PR * (2 * y + z_half), PR)
    picks = (
        lax.broadcasted_iota(jnp.int32, (PR, W), 1)
        == lax.broadcasted_iota(jnp.int32, (PR, W), 0) + strip_at
    ).astype(jnp.float32).astype(jnp.bfloat16)

    def gram_rows(blocks):
        for b in blocks:
            i, j = b // 8, b % 8
            g = whole[i * W : (i + 1) * W, j * W : (j + 1) * W]
            strip = whole[pl.ds(i * W + strip_at, PR), j * W : (j + 1) * W]
            both = nt(jnp.concatenate([strip, picks], axis=0), g)
            wide = nn(both[PR:].astype(jnp.bfloat16), g)
            for n, v in enumerate((both[:PR], wide)):
                v = jnp.where(z_odd == 1, v[8:], v[:8])
                grams[b, n] = jnp.concatenate([v[:, :PC], v[:, PC:]], axis=0).astype(jnp.bfloat16)

    def to_hub(src, dst, n):
        for t in FAR_Y:
            p = p0 if t % 2 == 0 else 1 - p0
            for b in (1 - z_half, z_half):
                block, h = 2 * ys[t] + b, ys[t] * ZS + 2 * b + p

                def remote(block=block, h=h):
                    pltpu.make_async_remote_copy(
                        src.at[block], dst.at[r], send_sem.at[n], recv_sem.at[n], **to(h)
                    ).start()

                if t == 0:
                    pl.when(h != r)(remote)

                    @pl.when(h == r)
                    def _(block=block):
                        pltpu.make_async_copy(src.at[block], dst.at[r], recv_sem.at[n]).start()
                else:
                    remote()

    loads[4].wait()
    gram_rows(range(0, 4))
    for n, (got, row, out) in enumerate(
        ((bases_in, bases_row, bases), (moments_in, moments_row, moments))
    ):
        wait_bytes(got, recv_sem.at[n])
        for b in range(KEPT):
            row[b] = got[idx(2 * SHARDS * CAP + KEPT + b)]
        to_hub(row, out, 2 + n)
        if n == 0:
            gram_rows(range(4, 9))

    def grams_to_owners():
        gram_rows(range(9, KEPT))
        for m in range(SHARDS * CAP):
            tsend[m] = grams[idx(m)]
        exchange(tsend, trecv, 5)

    pl.when(jnp.logical_not(is_hub))(grams_to_owners)

    block_me = 2 * y + z_half

    @pl.when(is_hub)
    def _():
        g = whole[
            pl.ds(pl.multiple_of(y // 4 * W, W), W),
            pl.ds(pl.multiple_of(y % 4 * (2 * W) + z_half * W, W), W),
        ]
        wait_bytes(bases, recv_sem.at[2])
        lb = unfold(bases[:, 0]).reshape(W, W).astype(jnp.bfloat16)
        rb = unfold(bases[:, 1]).reshape(W, W).astype(jnp.bfloat16)
        half = nn(lb, g).astype(jnp.bfloat16)
        turned = nn(half, rb)
        wait_bytes(moments, recv_sem.at[3])
        m0 = unfold(moments[:, 0]).reshape(W, W)
        v0 = unfold(moments[:, 1]).reshape(W, W)
        first = BETA_ONE * m0 + (1.0 - BETA_ONE) * turned
        second = BETA_TWO * v0 + (1.0 - BETA_TWO) * turned * turned
        scaled = (first / (jnp.sqrt(second) + EPSILON)).astype(jnp.bfloat16)
        back = nt(scaled, rb).astype(jnp.bfloat16)
        update[block_me] = tn(lb, back).astype(jnp.bfloat16)
        rsend[...] = fold(turned.reshape(REPS, 8, W))

    ups = (ys[1] * ZS + z, ys[7] * ZS + z)
    z_pair = 2 * z_half + 1 - z_odd
    z_next = jnp.where(z_odd == 1, zs[1], zs[3])
    pending = []
    names = {}

    def region(t, bit, rows):
        return update.at[2 * ys[t] + bit, pl.ds(rows[0], rows[1] - rows[0])]

    def push(ref, peer, key):
        n = names.setdefault(key, len(names))
        copy = pltpu.make_async_remote_copy(ref, ref, ag_send.at[n], ag_recv.at[n], **to(peer))
        copy.start()
        return copy

    def pull(ref, key):
        wait_bytes(ref, ag_recv.at[names[key]])

    bits = (z_half, 1 - z_half)
    parts = [(n * W // PARTS, (n + 1) * W // PARTS) for n in range(PARTS)]

    @pl.when(is_hub)
    def _():
        for n, (c, peer) in enumerate(((1, zs[2]), (1, z_next), (0, z_pair))):
            for m, rows in enumerate(parts):
                ref = region(0, bits[0], rows)
                key = names.setdefault(("z", c, m), len(names))
                pltpu.make_async_remote_copy(
                    ref, ref, z_send.at[3 * m + n], ag_recv.at[key], **to(y * ZS + peer)
                ).start()

    def y_rows(m, d, way):
        lo, hi = parts[m]
        if d < YS // 2:
            return lo, hi
        mid = (lo + hi) // 2
        return (lo, mid) if way == 0 else (mid, hi)

    def far(d, way):
        return (-d if way == 0 else d) % YS

    def y_push(c, m, d, way):
        ref = region(far(d - 1, way), bits[c], y_rows(m, d, way))
        pending.append(push(ref, ups[way], ("y", c, m, d, way)))

    def z_step(c, m):
        ref = region(0, bits[c], parts[m])
        if c == 0:
            pl.when(jnp.logical_not(is_hub))(lambda: pull(ref, ("z", c, m)))
        else:
            pull(ref, ("z", c, m))
        for way in range(2):
            y_push(c, m, 1, way)

    def y_step(c, m, d):
        for way in range(2):
            pull(region(far(d, way), bits[c], y_rows(m, d, way)), ("y", c, m, d, way))
            if d < YS // 2:
                y_push(c, m, d + 1, way)

    def send_r():
        @pl.when(is_hub)
        def _():
            for t in FAR_Y:
                for v in FAR_Z:
                    q = ys[t] * ZS + zs[v]
                    if t or v:
                        pltpu.make_async_remote_copy(
                            rsend.at[q], rbuf.at[block_me], send_sem.at[4], recv_sem.at[4], **to(q)
                        ).start()
                    else:
                        pltpu.make_async_copy(rsend.at[r], rbuf.at[block_me], recv_sem.at[4]).start()

    def to_owners():
        wait_bytes(rbuf, recv_sem.at[4])
        for m in range(SHARDS * CAP):
            r_send[m] = rbuf[idx(m)]
        exchange(r_send, r_recv, 6)

    def own_rows():
        wait_bytes(trecv, recv_sem.at[5])
        wait_bytes(r_recv, recv_sem.at[6])
        for copy in loads[5:7]:
            copy.wait()
        for n in range(KEPT):
            at = idx(SHARDS * CAP + n)
            gl, gr = unfold(trecv[at])
            turned = unfold(r_recv[pl.ds(at, 1)])[0]
            new_avg[n] = (BETA_ONE * avg[n].astype(jnp.float32) + (1.0 - BETA_ONE) * turned).astype(jnp.bfloat16)
            new_avg_sq[n] = BETA_TWO * avg_sq[n] + (1.0 - BETA_TWO) * turned * turned
            new_left[n] = BETA_TWO * left_gram[n] + (1.0 - BETA_TWO) * gl
            new_right[n] = BETA_TWO * right_gram[n] + (1.0 - BETA_TWO) * gr

    order = [(z_step, 0, m) for m in range(PARTS)]
    for m in range(PARTS):
        order += [(z_step, 1, m), (y_step, 0, m, 1)]
    order += [(y_step, 1, m, 1) for m in range(PARTS)]
    for d in (2, 3, 4):
        order += [(y_step, c, m, d) for c in (1, 0) for m in range(PARTS)]
    for count, (step, *args) in enumerate(order[:-2]):
        step(*args)
        if count == PARTS - 1:
            send_r()
            pl.when(is_hub)(grams_to_owners)
        if count == 4 * PARTS:
            to_owners()
        if count == len(order) - 4:
            own_rows()

    for copy in pending:
        copy.wait_send()
    for n, ref in ((0, bases_out), (1, moments_out), (5, tsend), (6, r_send)):
        wait_bytes(ref.at[pl.ds(0, CAP * (SHARDS - 1))], send_sem.at[n])

    @pl.when(is_hub)
    def _():
        wait_bytes(bases_row.at[pl.ds(0, KEPT - 1)], send_sem.at[2])
        wait_bytes(moments_row.at[pl.ds(0, KEPT - 1)], send_sem.at[3])
        wait_bytes(rsend.at[pl.ds(0, REPS - 1)], send_sem.at[4])
        for n in range(3 * PARTS):
            wait_bytes(region(0, bits[0], parts[n // 3]), z_send.at[n])

    @pl.when(jnp.logical_not(is_hub))
    def _():
        wait_bytes(bases_row, send_sem.at[2])
        wait_bytes(moments_row, send_sem.at[3])

    for step, *args in order[-2:]:
        step(*args)


def store_kernel(*refs):
    count = len(refs) // 2
    sems = refs[-1]
    copies = []
    for n in range(count):
        src, dst = refs[n], refs[count + n]
        if n == 0:
            for b in range(KEPT):
                i, j = b // 8, b % 8
                place = dst.at[i * W : (i + 1) * W, j * W : (j + 1) * W]
                copies.append(pltpu.make_async_copy(src.at[b], place, sems.at[len(copies)]))
        else:
            copies.append(pltpu.make_async_copy(src, dst, sems.at[len(copies)]))
    for copy in copies:
        copy.start()
    for copy in copies:
        copy.wait()


def body(grad, owner, left_basis, right_basis, avg, avg_sq, left_gram, right_gram):
    vmem = pl.BlockSpec(memory_space=pltpu.VMEM)
    hbm = pl.BlockSpec(memory_space=pltpu.HBM)
    bf16, f32 = jnp.bfloat16, jnp.float32
    slots = SHARDS * CAP
    rows = (KEPT, 8, W)
    outs = [jax.ShapeDtypeStruct(x.shape, x.dtype) for x in (grad, avg, avg_sq, left_gram, right_gram)]
    operands = [
        pltpu.with_memory_space_constraint(x, pltpu.HBM)
        for x in (owner.T, left_basis, right_basis, avg, avg_sq, grad, left_gram, right_gram)
    ]
    results = pl.pallas_call(
        kernel,
        out_shape=[jax.ShapeDtypeStruct((KEPT, W, W), bf16)] + outs[1:],
        in_specs=[hbm] * 8,
        out_specs=[vmem] * 5,
        scratch_shapes=[
            pltpu.VMEM(owner.shape[::-1], jnp.int32),
            pltpu.VMEM((8, 128), jnp.int32),
            pltpu.SMEM((8, 128), jnp.int32),
            pltpu.VMEM(rows, bf16),
            pltpu.VMEM(rows, bf16),
            pltpu.VMEM(rows, bf16),
            pltpu.VMEM(rows, f32),
            pltpu.VMEM(grad.shape, bf16),
            pltpu.VMEM(rows, f32),
            pltpu.VMEM(rows, f32),
            pltpu.VMEM((KEPT, 2, PR, PC), bf16),
            pltpu.VMEM((slots, 2, PR, PC), bf16),
            pltpu.VMEM((slots, 2, PR, PC), bf16),
            pltpu.VMEM((slots, 2, PR, PC), bf16),
            pltpu.VMEM((slots, 2, PR, PC), bf16),
            pltpu.VMEM((KEPT, 2, PR, PC), bf16),
            pltpu.VMEM((KEPT, 2, PR, PC), bf16),
            pltpu.VMEM((REPS, 2, PR, PC), bf16),
            pltpu.VMEM((REPS, 2, PR, PC), bf16),
            pltpu.VMEM((REPS, PR, PC), bf16),
            pltpu.VMEM((KEPT, PR, PC), bf16),
            pltpu.VMEM((KEPT, 2, PR, PC), bf16),
            pltpu.VMEM((slots, 2, PR, PC), bf16),
            pltpu.VMEM((slots, 2, PR, PC), bf16),
            pltpu.VMEM((slots, PR, PC), bf16),
            pltpu.VMEM((slots, PR, PC), bf16),
            pltpu.SemaphoreType.DMA((8,)),
            pltpu.SemaphoreType.DMA,
            pltpu.SemaphoreType.DMA((7,)),
            pltpu.SemaphoreType.DMA((7,)),
            pltpu.SemaphoreType.DMA((3 * PARTS,)),
            pltpu.SemaphoreType.DMA((18 * PARTS,)),
            pltpu.SemaphoreType.DMA((18 * PARTS,)),
        ],
        compiler_params=pltpu.CompilerParams(
            collective_id=0, has_side_effects=True, vmem_limit_bytes=40 * 1024 * 1024
        ),
        cost_estimate=pl.CostEstimate(flops=12 * W**3, bytes_accessed=6 << 20, transcendentals=0),
        name="soap_step",
    )(*operands)
    return tuple(
        pl.pallas_call(
            store_kernel,
            out_shape=outs,
            in_specs=[pl.BlockSpec(memory_space=pl.ANY)] * 5,
            out_specs=[hbm] * 5,
            scratch_shapes=[pltpu.SemaphoreType.DMA((KEPT + 4,))],
            compiler_params=pltpu.CompilerParams(vmem_limit_bytes=4 * 1024 * 1024),
            cost_estimate=pl.CostEstimate(flops=0, bytes_accessed=5 << 20, transcendentals=0),
            name="store",
        )(*results)
    )


def solution(mesh):
    rows = P("shard", "rep", None)
    return jax.shard_map(
        body,
        mesh=mesh,
        in_specs=(P("shard", None), P(), rows, rows, rows, rows, rows, rows),
        out_specs=(P("shard", None), rows, rows, rows, rows),
        check_vma=False,
    )
```
